32 devices in a mesh: tile: 8 (over y, x, core), chan: 4 (over z).
Axes of the slice: x: 2, y: 2, z: 4, core: 2. Of those that a mesh axis runs over, the one named last changes fastest.
Arguments:
- points: bfloat16 [128, 8192], P('chan', 'tile'), may hold values from -6 to 6
- dest: int32 [8192, 1], P('tile'), may hold values from 0 to 7; in each aligned block of 1024 rows (0 to 1023, 1024 to 2047, ...) at most 384 rows name the same one
- voxel: int32 [8192, 1], P('tile'), may hold values from 0 to 2047
- weight: bfloat16 [256, 27, 128], P('chan'), may hold values from -0.109375 to 0.109375
- grad_out: bfloat16 [256, 16384], P('chan', 'tile'), may hold values from -6 to 6
Outputs:
- features_out: bfloat16 [256, 16384], P('chan', 'tile')
- weight_grad: float32 [256, 3456], P('chan', 'tile')
The draws below stay inside these ranges and needn't reach their ends.
Inputs may be any that keep to these rules, and one draw needn't show every extreme that they name: `dest`: among the 1024 points of one scene owner (aligned blocks of rows), at most 384 go to any one tile, and some tile receives exactly 384 of them.
All inputs are finite; a program needn't handle non-finite values.
Results may differ from the reference program's by a relative error of at most 0.0029.
Values may be sent and summed in bfloat16 or wider, within the bound.
A program may use at most 64 MiB of HBM per device.

```python
import math
import jax
import jax.numpy as jnp
import numpy as np
from jax import lax

C_IN = 128
C_OUT = 256
EDGE = 16
DEPTH = 8
PTS_DEV = 1024
VOX = 2048
TILES = 8
POINTS = 8192
CAP = 384


def place_ends(values, own_key, low, largest):
    spot = [jax.random.randint(jax.random.fold_in(own_key, axis), (), 0, length) for axis, length in enumerate(values.shape)]
    widest = values.shape.index(max(values.shape))
    neighbour = spot[:widest] + [(spot[widest] + 1) % values.shape[widest]] + spot[widest + 1:]
    return values.at[tuple(spot)].set(low).at[tuple(neighbour)].set(largest)


def block_scale(stream_key, shape, pieces, smallest, high):
    level, own = 1.0, jax.random.fold_in(stream_key, 6)
    for dim, shards_of in pieces:
        steps = jnp.exp(jax.random.uniform(jax.random.fold_in(own, dim), (shards_of,), jnp.float32, smallest / len(pieces), high / len(pieces)))
        level = level * jnp.repeat(steps, shape[dim] // shards_of).reshape([-1 if axis == dim else 1 for axis in range(len(shape))])
    return level


def shared_out(key, own, number, rows, amount, top, limit, lean):
    sequence = jax.random.permutation(key, amount)
    packed, common = portions_of(amount, rows * top, limit, lean, True), portions_of(amount, rows * top, limit, lean, False)
    places = jnp.arange(amount)

    def named(lengths, rotation):
        used = int((lengths > 0).sum())
        fixed = max(1, used // 4)
        shifted = fixed + (places - fixed + rotation * (used - fixed)) % max(1, amount - fixed)
        return jnp.zeros((amount,), jnp.int32).at[sequence[jnp.where(places < fixed, places, shifted)]].set(jnp.asarray(lengths, jnp.int32))

    lengths = jnp.where(number % 4 == 0, named(packed, number // 4), named(common, number - number // 4 - 1))
    mixed = jax.random.permutation(jax.random.fold_in(own, 3), amount)
    donor, taker = mixed[0:amount // 2 * 2:2], mixed[1:amount // 2 * 2:2]
    slack = jnp.minimum(lengths[donor] - 1, limit - lengths[taker]) // 2
    slack = jnp.where((donor == sequence[0]) | (taker == sequence[0]) | (lengths[taker] == 0), 0, jnp.maximum(slack, 0))
    shifted = jax.random.randint(jax.random.fold_in(own, 4), (amount // 2,), 0, 1 << 20) % (slack + 1)
    lengths = lengths.at[donor].add(-shifted).at[taker].add(shifted)
    items = jnp.searchsorted(jnp.cumsum(lengths), jnp.arange(rows * top), side="right").astype(jnp.int32)
    table = items.reshape(top, rows).T
    table = table[jax.random.permutation(jax.random.fold_in(own, 1), rows)]
    rotation = jax.random.randint(jax.random.fold_in(own, 2), (rows, 1), 0, top)
    return jnp.take_along_axis(table, (jnp.arange(top)[None, :] + rotation) % top, axis=1)


def portions_of(count, total, limit, lean, full):
    weights = [(1 << 20) // math.isqrt(rank ** lean) + 1 for rank in range(1, count + 1)]
    largest = limit if full else min(limit, max(-(-total // count), total * weights[0] // sum(weights)))
    least = 1 if total - largest >= count - 1 else 0
    given, rest = [largest] + [least] * (count - 1), total - largest - least * (count - 1)
    while rest > 0:
        free = [i for i in range(1, count) if given[i] < largest] or [i for i in range(1, count) if given[i] < limit]
        pool, remaining = sum([weights[i] for i in free]), rest
        for i in free:
            addition = min(limit - given[i], max(1, remaining * weights[i] // pool), rest)
            given[i] = given[i] + addition
            rest = rest - addition
    return np.array(given)


def bell_draw(rng, extent, scale, most, shards=(), held_as=jnp.bfloat16):
    entries = scale * jax.random.normal(rng, extent, jnp.float32)
    if shards:
        entries = entries * block_scale(rng, extent, shards, -0.22, 0.18)
    return jnp.clip(entries, -most, most).astype(held_as)


def setup_inputs(seed: int = 0) -> dict:
    streams_of = jax.random.split(jax.random.key(seed), 6)
    points = bell_draw(streams_of[0], (C_IN, POINTS), 1.0, 6.0, ((0, 4), (1, 8)))
    dest_keys = jax.random.split(jax.random.fold_in(streams_of[1], 1), POINTS // PTS_DEV)
    dest_turns = jax.random.permutation(jax.random.fold_in(streams_of[1], 3), POINTS // PTS_DEV)
    dest = jax.vmap(lambda own, number: shared_out(jax.random.fold_in(streams_of[1], 2), own, number, PTS_DEV, TILES, 1, CAP, 2))(dest_keys, dest_turns).reshape((POINTS, 1))
    voxel = place_ends(jax.random.randint(streams_of[2], (POINTS, 1), 0, VOX), jax.random.fold_in(streams_of[2], 1), 0, VOX - 1).astype(jnp.int32)
    weight = bell_draw(streams_of[3], (C_OUT, 27, C_IN), (27 * C_IN) ** -0.5, 0.109375, ((0, 4),))
    grad_out = bell_draw(streams_of[4], (C_OUT, TILES * VOX), 1.0, 6.0, ((0, 4), (1, 8)))
    return {"points": points, "dest": dest, "voxel": voxel, "weight": weight, "grad_out": grad_out}


def tile_conv(grid_part, weight_part, masked):
    count = grid_part.shape[0]
    cube = grid_part.reshape(count, DEPTH, EDGE, EDGE)
    padded = jnp.pad(cube, ((0, 0), (1, 1), (1, 1), (1, 1)))
    output = jnp.zeros((weight_part.shape[0], DEPTH * EDGE * EDGE), jnp.float32)
    grads = []
    for index in range(27):
        first, second, third = index // 9, (index // 3) % 3, index % 3
        moved = padded[:, first:first + DEPTH, second:second + EDGE, third:third + EDGE].reshape(count, DEPTH * EDGE * EDGE)
        output = output + jnp.dot(weight_part[:, index, :], moved, preferred_element_type=jnp.float32)
        grads.append(lax.dot_general(masked, moved, (((1,), (1,)), ((), ())), preferred_element_type=jnp.float32))
    return output, jnp.stack(grads, axis=1)


def reference(points, dest, voxel, weight, grad_out):
    cell = dest[:, 0].astype(jnp.int32) * VOX + voxel[:, 0].astype(jnp.int32)
    sums = jax.ops.segment_sum(points.astype(jnp.float32).T, cell, num_segments=TILES * VOX)
    counts = jax.ops.segment_sum(jnp.ones(cell.shape, jnp.float32), cell, num_segments=TILES * VOX)
    grid = (sums / jnp.maximum(counts, 1.0)[:, None]).astype(jnp.bfloat16)
    grid = grid.reshape(TILES, VOX, C_IN).transpose(0, 2, 1)
    occupied = (counts > 0).astype(jnp.float32).reshape(TILES, VOX)
    cotangent = grad_out.reshape(C_OUT, TILES, VOX).transpose(1, 0, 2)

    def one_tile(total, items):
        grid_tile, mask_tile, cot_tile = items
        masked = (cot_tile.astype(jnp.float32) * mask_tile[None, :]).astype(jnp.bfloat16)
        output, grads = tile_conv(grid_tile, weight, masked)
        return total + grads, (output * mask_tile[None, :]).astype(jnp.bfloat16)

    total, outputs = lax.scan(one_tile, jnp.zeros((C_OUT, 27, C_IN), jnp.float32), (grid, occupied, cotangent))
    features_out = outputs.transpose(1, 0, 2).reshape(C_OUT, TILES * VOX)
    return features_out, total.reshape(C_OUT, 27 * C_IN)
```

```python
import functools

import jax
import jax.numpy as jnp
from jax import lax
from jax.experimental import pallas as pl
from jax.experimental.pallas import tpu as pltpu
from jax.sharding import PartitionSpec as P

EDGE = 16
DEPTH = 8
PLANE = EDGE * EDGE
VOX = DEPTH * PLANE
PADDED = PLANE + 2 * EDGE
CHUNKS = 4
PER_CHUNK = DEPTH // CHUNKS
ROWS_MAJOR = (((1,), (1,)), ((), ()))


def repeat(start, stop, body):
    if stop - start <= 8:
        for step in range(start, stop):
            body(step)
    else:
        lax.fori_loop(start, stop, lambda step, carry: (body(step), carry)[1], 0)


def kernel(
    tiles,
    chans,
    width,
    pts_ref,
    dest_ref,
    voxel_ref,
    weight_ref,
    grad_ref,
    out_ref,
    wgrad_ref,
    codes,
    pts_all,
    sums,
    grid,
    shifts,
    moved,
    taps,
    masked,
    partial,
    total,
    sending,
    received,
    pts_send,
    pts_recv,
    code_send,
    code_recv,
    grid_send,
    grid_recv,
    grad_send,
    grad_recv,
):
    me = lax.axis_index("tile")
    mine = lax.axis_index("chan")
    part = pts_ref.shape[0]
    outs = grad_ref.shape[0]
    channels = part * chans
    span = sending.shape[2]

    def peer(step):
        return lax.rem(me + step, tiles)

    def giver(step):
        return lax.rem(me + tiles - step, tiles)

    def chan_peer(step):
        return lax.rem(mine + step, chans)

    barrier = pltpu.get_barrier_semaphore()

    def greet(step):
        pl.semaphore_signal(barrier, inc=1, device_id={"tile": peer(step)})

    def greet_chan(step):
        pl.semaphore_signal(barrier, inc=1, device_id={"chan": chan_peer(step)})

    repeat(1, tiles, greet)
    repeat(1, chans, greet_chan)
    codes[me] = dest_ref[...] * VOX + voxel_ref[...]
    pl.semaphore_wait(barrier, tiles + chans - 2)

    def code_copy(step):
        return pltpu.make_async_remote_copy(
            src_ref=codes.at[me],
            dst_ref=codes.at[me],
            send_sem=code_send.at[step],
            recv_sem=code_recv.at[step],
            device_id={"tile": peer(step)},
        )

    def pts_copy(step):
        return pltpu.make_async_remote_copy(
            src_ref=pts_ref,
            dst_ref=pts_all.at[me],
            send_sem=pts_send.at[step],
            recv_sem=pts_recv.at[step],
            device_id={"tile": peer(step)},
        )

    def send_points(step):
        code_copy(step).start()
        pts_copy(step).start()

    repeat(1, tiles, send_points)

    for a in range(3):
        for tap in range(9):
            taps[a * outs : (a + 1) * outs, tap * channels : (tap + 1) * channels] = weight_ref[
                9 * a + tap
            ]
    to = lax.broadcasted_iota(jnp.int32, (PLANE, PLANE), 0)
    source = lax.broadcasted_iota(jnp.int32, (PLANE, PLANE), 1)
    for e in (-1, 0, 1):
        line = (to & (EDGE - 1)) + e
        here = (source == to + e) & (line >= 0) & (line < EDGE)
        shifts[(e + 1) * PLANE : (e + 2) * PLANE, :] = here.astype(jnp.float32).astype(jnp.bfloat16)
    edge = jnp.zeros((EDGE, moved.shape[2]), jnp.bfloat16)
    for plane in range(DEPTH):
        moved[plane, :EDGE, :] = edge
        moved[plane, PADDED - EDGE :, :] = edge
    masked[0] = jnp.zeros((outs, PLANE), jnp.bfloat16)
    masked[DEPTH + 1] = jnp.zeros((outs, PLANE), jnp.bfloat16)

    def add_points(features, code):
        rel = code - me * VOX
        high = rel >> 8
        low = rel & (PLANE - 1)
        count = features.shape[1]
        wide = features.astype(jnp.float32)
        rows = [jnp.where(high == h, wide, 0.0).astype(jnp.bfloat16) for h in range(DEPTH)]
        rank = lax.broadcasted_iota(jnp.int32, (2 * DEPTH, count), 0)
        rows.append((rank == high).astype(jnp.float32).astype(jnp.bfloat16))
        cell = lax.broadcasted_iota(jnp.int32, (PLANE, count), 0)
        onehot = (cell == low).astype(jnp.float32).astype(jnp.bfloat16)
        return lax.dot_general(
            jnp.concatenate(rows, axis=0), onehot, ROWS_MAJOR, preferred_element_type=jnp.float32
        )

    sums[...] = add_points(pts_ref[...], codes[me])

    def take_points(step):
        code_copy(step).wait_recv()
        pts_copy(step).wait_recv()
        origin = giver(step)
        sums[...] += add_points(pts_all[origin], codes[origin])

    repeat(1, tiles, take_points)

    counts = sums[DEPTH * part : DEPTH * part + DEPTH, :]
    floor = jnp.maximum(counts, 1.0)
    occupied = (counts > 0).astype(jnp.float32)
    held = grid.shape[2]

    def grid_copy(chunk, step):
        planes = pl.ds(chunk * PER_CHUNK, PER_CHUNK)
        return pltpu.make_async_remote_copy(
            src_ref=grid.at[planes, mine],
            dst_ref=grid.at[planes, mine],
            send_sem=grid_send.at[chunk, step],
            recv_sem=grid_recv.at[chunk, step],
            device_id={"chan": chan_peer(step)},
        )

    for chunk in range(CHUNKS):
        for plane in range(chunk * PER_CHUNK, (chunk + 1) * PER_CHUNK):
            mean = sums[plane * part : (plane + 1) * part, :] / floor[plane : plane + 1, :]
            if held > part:
                mean = jnp.concatenate([mean, jnp.zeros((held - part, PLANE), jnp.float32)], axis=0)
            grid[plane, mine] = mean.astype(jnp.bfloat16)
        for step in range(1, chans):
            grid_copy(chunk, step).start()

    for plane in range(DEPTH):
        kept = grad_ref[:, plane * PLANE : (plane + 1) * PLANE].astype(jnp.float32)
        masked[plane + 1] = (kept * occupied[plane : plane + 1, :]).astype(jnp.bfloat16)

    for chunk in range(CHUNKS):
        for step in range(1, chans):
            grid_copy(chunk, step).wait_recv()
        for plane in range(chunk * PER_CHUNK, (chunk + 1) * PER_CHUNK):
            if held > part:
                lanes = [grid[plane, c].astype(jnp.float32)[:part] for c in range(chans)]
                voxels = jnp.concatenate(lanes, axis=0).astype(jnp.bfloat16)
            else:
                voxels = grid[plane].reshape(channels, PLANE)
            lines = lax.dot_general(
                shifts[...], voxels, ROWS_MAJOR, preferred_element_type=jnp.float32
            ).astype(jnp.bfloat16)
            for e in range(3):
                moved[plane, EDGE : EDGE + PLANE, e * channels : (e + 1) * channels] = lines[
                    e * PLANE : (e + 1) * PLANE, :
                ]
            columns = jnp.concatenate(
                [moved[plane, b * EDGE : b * EDGE + PLANE, :] for b in range(3)], axis=1
            )
            partial[plane] = lax.dot_general(
                taps[...], columns, ROWS_MAJOR, preferred_element_type=jnp.float32
            )
            cotangents = jnp.concatenate([masked[plane + 2], masked[plane + 1], masked[plane]], axis=0)
            grads = jnp.dot(cotangents, columns, preferred_element_type=jnp.float32)
            for a in range(3):
                place = slice(a * 9 * channels, (a + 1) * 9 * channels)
                piece = grads[a * outs : (a + 1) * outs, :]
                if plane == 0:
                    total[:, place] = piece
                else:
                    total[:, place] += piece
    total[:, 27 * channels :] = jnp.zeros((outs, total.shape[1] - 27 * channels), jnp.float32)

    def block(owner):
        first = owner * width
        base = pl.multiple_of(first // 128 * 128, 128)
        window = total[:, pl.ds(base, span + 128)]
        return pltpu.roll(window, span + 128 - lax.rem(first, 128), 1)[:, :span]

    def grad_copy(step):
        return pltpu.make_async_remote_copy(
            src_ref=sending.at[step],
            dst_ref=received.at[step],
            send_sem=grad_send.at[step],
            recv_sem=grad_recv.at[step],
            device_id={"tile": peer(step)},
        )

    def send_grads(step):
        sending[step] = block(peer(step)).astype(jnp.bfloat16)
        grad_copy(step).start()

    repeat(1, tiles, send_grads)

    for plane in range(DEPTH):
        output = partial[plane, outs : 2 * outs, :]
        if plane > 0:
            output = output + partial[plane - 1, :outs, :]
        if plane < DEPTH - 1:
            output = output + partial[plane + 1, 2 * outs :, :]
        out_ref[:, plane * PLANE : (plane + 1) * PLANE] = (
            output * occupied[plane : plane + 1, :]
        ).astype(jnp.bfloat16)

    total[:, :span] = block(me)

    def take_grads(step):
        grad_copy(step).wait_recv()
        total[:, :span] += received[step].astype(jnp.float32)

    repeat(1, tiles, take_grads)
    wgrad_ref[...] = total[:, :width]

    def sent(step):
        code_copy(step).wait_send()
        pts_copy(step).wait_send()
        grad_copy(step).wait_send()

    repeat(1, tiles, sent)
    for chunk in range(CHUNKS):
        for step in range(1, chans):
            grid_copy(chunk, step).wait_send()


def on_device(points, dest, voxel, weight, grad_out):
    tiles, chans = lax.axis_size("tile"), lax.axis_size("chan")
    part, count = points.shape
    outs = grad_out.shape[0]
    channels = part * chans
    width = 27 * channels // tiles
    span = -(-width // 128) * 128
    total_width = max(((tiles - 1) * width // 128) * 128 + span + 128, 27 * channels + 128)
    vmem = pl.BlockSpec(memory_space=pltpu.VMEM)
    dma = pltpu.SemaphoreType.DMA
    return pl.pallas_call(
        functools.partial(kernel, tiles, chans, width),
        out_shape=(
            jax.ShapeDtypeStruct((outs, VOX), jnp.bfloat16),
            jax.ShapeDtypeStruct((outs, width), jnp.float32),
        ),
        in_specs=[vmem] * 5,
        out_specs=(vmem, vmem),
        scratch_shapes=[
            pltpu.VMEM((tiles, 1, count), jnp.int32),
            pltpu.VMEM((tiles, part, count), jnp.bfloat16),
            pltpu.VMEM((DEPTH * part + 2 * DEPTH, PLANE), jnp.float32),
            pltpu.VMEM((DEPTH, chans, max(part, 16), PLANE), jnp.bfloat16),
            pltpu.VMEM((3 * PLANE, PLANE), jnp.bfloat16),
            pltpu.VMEM((DEPTH, PADDED, 3 * channels), jnp.bfloat16),
            pltpu.VMEM((3 * outs, 9 * channels), jnp.bfloat16),
            pltpu.VMEM((DEPTH + 2, outs, PLANE), jnp.bfloat16),
            pltpu.VMEM((DEPTH, 3 * outs, PLANE), jnp.float32),
            pltpu.VMEM((outs, total_width), jnp.float32),
            pltpu.VMEM((tiles, outs, span), jnp.bfloat16),
            pltpu.VMEM((tiles, outs, span), jnp.bfloat16),
            dma((tiles,)),
            dma((tiles,)),
            dma((tiles,)),
            dma((tiles,)),
            dma((CHUNKS, chans)),
            dma((CHUNKS, chans)),
            dma((tiles,)),
            dma((tiles,)),
        ],
        compiler_params=pltpu.CompilerParams(
            collective_id=0, has_side_effects=True, vmem_limit_bytes=40 * 1024 * 1024
        ),
    )(
        points,
        dest.reshape(1, count),
        voxel.reshape(1, count),
        jnp.transpose(weight, (1, 0, 2)),
        grad_out,
    )


def solution(mesh):
    placed = (
        P("chan", "tile"),
        P("tile", None),
        P("tile", None),
        P("chan", None, None),
        P("chan", "tile"),
    )
    return jax.shard_map(
        on_device,
        mesh=mesh,
        in_specs=placed,
        out_specs=(P("chan", "tile"), P("chan", "tile")),
        check_vma=False,
    )
```

```python
import functools

import jax
import jax.numpy as jnp
from jax import lax
from jax.experimental import pallas as pl
from jax.experimental.pallas import tpu as pltpu
from jax.sharding import PartitionSpec as P

EDGE = 16
DEPTH = 8
PLANE = EDGE * EDGE
VOX = DEPTH * PLANE
PADDED = PLANE + 2 * EDGE
CHUNKS = 4
PER_CHUNK = DEPTH // CHUNKS
ROWS_MAJOR = (((1,), (1,)), ((), ()))


def repeat(start, stop, body):
    if stop - start <= 8:
        for step in range(start, stop):
            body(step)
    else:
        lax.fori_loop(start, stop, lambda step, carry: (body(step), carry)[1], 0)


def kernel(
    tiles,
    chans,
    width,
    pts_ref,
    dest_ref,
    voxel_ref,
    weight_ref,
    grad_ref,
    out_ref,
    wgrad_ref,
    dest_here,
    voxel_here,
    weight_here,
    grad_here,
    codes,
    pts_all,
    sums,
    grid,
    shifts,
    moved,
    taps,
    masked,
    partial,
    total,
    handing,
    handed,
    sending,
    received,
    local_sem,
    pts_send,
    pts_recv,
    share_send,
    share_recv,
    code_send,
    code_recv,
    grid_send,
    grid_recv,
    hand_send,
    hand_recv,
    grad_send,
    grad_recv,
):
    me = lax.axis_index("tile")
    mine = lax.axis_index("chan")
    part = pts_ref.shape[0]
    outs = grad_ref.shape[0]
    channels = part * chans
    span = sending.shape[2]
    chips = tiles // 2
    chip, core = me // 2, lax.rem(me, 2)
    sibling = 2 * chip + 1 - core

    def peer(step):
        return lax.rem(me + step, tiles)

    def giver(step):
        return lax.rem(me + tiles - step, tiles)

    def chip_peer(step):
        return lax.rem(chip + step, chips)

    def chip_giver(step):
        return lax.rem(chip + chips - step, chips)

    def chan_peer(step):
        return lax.rem(mine + step, chans)

    barrier = pltpu.get_barrier_semaphore()

    def greet(step):
        pl.semaphore_signal(barrier, inc=1, device_id={"tile": peer(step)})

    def greet_chan(step):
        pl.semaphore_signal(barrier, inc=1, device_id={"chan": chan_peer(step)})

    def local(place, source, target):
        return pltpu.make_async_copy(source, target, local_sem.at[place])

    fetched = [
        local(0, dest_ref, dest_here),
        local(1, voxel_ref, voxel_here),
        local(2, pts_ref, pts_all.at[me]),
        local(3, weight_ref, weight_here),
        local(4, grad_ref, grad_here),
    ]
    for copy in fetched:
        copy.start()
    repeat(1, tiles, greet)
    repeat(1, chans, greet_chan)
    fetched[0].wait()
    fetched[1].wait()
    codes[me] = dest_here[...] * VOX + voxel_here[...]
    pl.semaphore_wait(barrier, tiles + chans - 2)

    def code_copy(step):
        return pltpu.make_async_remote_copy(
            src_ref=codes.at[me],
            dst_ref=codes.at[me],
            send_sem=code_send.at[step],
            recv_sem=code_recv.at[step],
            device_id={"tile": peer(step)},
        )

    def pts_copy(step):
        return pltpu.make_async_remote_copy(
            src_ref=pts_ref,
            dst_ref=pts_all.at[me],
            send_sem=pts_send.at[step],
            recv_sem=pts_recv.at[step],
            device_id={"tile": 2 * chip_peer(step) + core},
        )

    def share_copy(step):
        origin = 2 * chip_giver(step) + core
        return pltpu.make_async_remote_copy(
            src_ref=pts_all.at[origin],
            dst_ref=pts_all.at[origin],
            send_sem=share_send.at[step],
            recv_sem=share_recv.at[step],
            device_id={"tile": sibling},
        )

    repeat(1, chips, lambda step: pts_copy(step).start())
    repeat(1, tiles, lambda step: code_copy(step).start())
    fetched[2].wait()
    share_copy(0).start()
    fetched[3].wait()

    for a in range(3):
        for tap in range(9):
            taps[a * outs : (a + 1) * outs, tap * channels : (tap + 1) * channels] = weight_here[
                9 * a + tap
            ]
    to = lax.broadcasted_iota(jnp.int32, (PLANE, PLANE), 0)
    source = lax.broadcasted_iota(jnp.int32, (PLANE, PLANE), 1)
    for e in (-1, 0, 1):
        line = (to & (EDGE - 1)) + e
        here = (source == to + e) & (line >= 0) & (line < EDGE)
        shifts[(e + 1) * PLANE : (e + 2) * PLANE, :] = here.astype(jnp.float32).astype(jnp.bfloat16)
    edge = jnp.zeros((EDGE, moved.shape[2]), jnp.bfloat16)
    for plane in range(DEPTH):
        moved[plane, :EDGE, :] = edge
        moved[plane, PADDED - EDGE :, :] = edge
    masked[0] = jnp.zeros((outs, PLANE), jnp.bfloat16)
    masked[DEPTH + 1] = jnp.zeros((outs, PLANE), jnp.bfloat16)

    def add_points(features, code):
        rel = code - me * VOX
        high = rel >> 8
        low = rel & (PLANE - 1)
        count = features.shape[1]
        wide = features.astype(jnp.float32)
        rows = [jnp.where(high == h, wide, 0.0).astype(jnp.bfloat16) for h in range(DEPTH)]
        rank = lax.broadcasted_iota(jnp.int32, (2 * DEPTH, count), 0)
        rows.append((rank == high).astype(jnp.float32).astype(jnp.bfloat16))
        cell = lax.broadcasted_iota(jnp.int32, (PLANE, count), 0)
        onehot = (cell == low).astype(jnp.float32).astype(jnp.bfloat16)
        return lax.dot_general(
            jnp.concatenate(rows, axis=0), onehot, ROWS_MAJOR, preferred_element_type=jnp.float32
        )

    sums[...] = add_points(pts_all[me], codes[me])
    repeat(1, tiles, lambda step: code_copy(step).wait_recv())

    def take_points(origin):
        sums[...] += add_points(pts_all[origin], codes[origin])

    def take_shared(step):
        share_copy(step).wait_recv()
        take_points(2 * chip_giver(step) + 1 - core)

    def take_sent(step):
        pts_copy(step).wait_recv()
        share_copy(step).start()
        take_points(2 * chip_giver(step) + core)

    take_shared(0)
    repeat(1, chips, take_sent)
    repeat(1, chips, take_shared)

    counts = sums[DEPTH * part : DEPTH * part + DEPTH, :]
    floor = jnp.maximum(counts, 1.0)
    occupied = (counts > 0).astype(jnp.float32)
    held = grid.shape[2]

    def grid_copy(chunk, step):
        planes = pl.ds(chunk * PER_CHUNK, PER_CHUNK)
        return pltpu.make_async_remote_copy(
            src_ref=grid.at[planes, mine],
            dst_ref=grid.at[planes, mine],
            send_sem=grid_send.at[chunk, step],
            recv_sem=grid_recv.at[chunk, step],
            device_id={"chan": chan_peer(step)},
        )

    for chunk in range(CHUNKS):
        for plane in range(chunk * PER_CHUNK, (chunk + 1) * PER_CHUNK):
            mean = sums[plane * part : (plane + 1) * part, :] / floor[plane : plane + 1, :]
            if held > part:
                mean = jnp.concatenate([mean, jnp.zeros((held - part, PLANE), jnp.float32)], axis=0)
            grid[plane, mine] = mean.astype(jnp.bfloat16)
        for step in range(1, chans):
            grid_copy(chunk, step).start()

    fetched[4].wait()
    for plane in range(DEPTH):
        kept = grad_here[:, plane * PLANE : (plane + 1) * PLANE].astype(jnp.float32)
        masked[plane + 1] = (kept * occupied[plane : plane + 1, :]).astype(jnp.bfloat16)

    for chunk in range(CHUNKS):
        for step in range(1, chans):
            grid_copy(chunk, step).wait_recv()
        for plane in range(chunk * PER_CHUNK, (chunk + 1) * PER_CHUNK):
            if held > part:
                lanes = [grid[plane, c].astype(jnp.float32)[:part] for c in range(chans)]
                voxels = jnp.concatenate(lanes, axis=0).astype(jnp.bfloat16)
            else:
                voxels = grid[plane].reshape(channels, PLANE)
            lines = lax.dot_general(
                shifts[...], voxels, ROWS_MAJOR, preferred_element_type=jnp.float32
            ).astype(jnp.bfloat16)
            for e in range(3):
                moved[plane, EDGE : EDGE + PLANE, e * channels : (e + 1) * channels] = lines[
                    e * PLANE : (e + 1) * PLANE, :
                ]
            columns = jnp.concatenate(
                [moved[plane, b * EDGE : b * EDGE + PLANE, :] for b in range(3)], axis=1
            )
            partial[plane] = lax.dot_general(
                taps[...], columns, ROWS_MAJOR, preferred_element_type=jnp.float32
            )
            cotangents = jnp.concatenate([masked[plane + 2], masked[plane + 1], masked[plane]], axis=0)
            grads = jnp.dot(cotangents, columns, preferred_element_type=jnp.float32)
            for a in range(3):
                place = slice(a * 9 * channels, (a + 1) * 9 * channels)
                piece = grads[a * outs : (a + 1) * outs, :]
                if plane == 0:
                    total[:, place] = piece
                else:
                    total[:, place] += piece
    total[:, 27 * channels :] = jnp.zeros((outs, total.shape[1] - 27 * channels), jnp.float32)

    def block(owner):
        first = owner * width
        base = pl.multiple_of(first // 128 * 128, 128)
        window = total[:, pl.ds(base, span + 128)]
        return pltpu.roll(window, span + 128 - lax.rem(first, 128), 1)[:, :span]

    def hand_copy(step):
        return pltpu.make_async_remote_copy(
            src_ref=handing.at[step],
            dst_ref=handed.at[step],
            send_sem=hand_send.at[step],
            recv_sem=hand_recv.at[step],
            device_id={"tile": sibling},
        )

    def grad_copy(step):
        return pltpu.make_async_remote_copy(
            src_ref=sending.at[step],
            dst_ref=received.at[step],
            send_sem=grad_send.at[step],
            recv_sem=grad_recv.at[step],
            device_id={"tile": 2 * chip_peer(step) + core},
        )

    def hand_grads(step):
        handing[step] = block(2 * chip_peer(step) + 1 - core)
        hand_copy(step).start()

    def send_grads(step):
        own = block(2 * chip_peer(step) + core)
        hand_copy(step).wait_recv()
        sending[step] = (own + handed[step]).astype(jnp.bfloat16)
        grad_copy(step).start()

    repeat(1, chips, hand_grads)
    hand_grads(0)
    repeat(1, chips, send_grads)

    for plane in range(DEPTH):
        output = partial[plane, outs : 2 * outs, :]
        if plane > 0:
            output = output + partial[plane - 1, :outs, :]
        if plane < DEPTH - 1:
            output = output + partial[plane + 1, 2 * outs :, :]
        out_ref[:, plane * PLANE : (plane + 1) * PLANE] = (
            output * occupied[plane : plane + 1, :]
        ).astype(jnp.bfloat16)

    own_block = block(me)
    hand_copy(0).wait_recv()
    total[:, :span] = own_block + handed[0]

    def take_grads(step):
        grad_copy(step).wait_recv()
        total[:, :span] += received[step].astype(jnp.float32)

    repeat(1, chips, take_grads)
    wgrad_ref[...] = total[:, :width]

    def sent(step):
        pts_copy(step).wait_send()
        grad_copy(step).wait_send()

    def handed_over(step):
        share_copy(step).wait_send()
        hand_copy(step).wait_send()

    repeat(1, tiles, lambda step: code_copy(step).wait_send())
    repeat(1, chips, sent)
    repeat(0, chips, handed_over)
    for chunk in range(CHUNKS):
        for step in range(1, chans):
            grid_copy(chunk, step).wait_send()


def on_device(points, dest, voxel, weight, grad_out):
    tiles, chans = lax.axis_size("tile"), lax.axis_size("chan")
    part, count = points.shape
    outs = grad_out.shape[0]
    channels = part * chans
    width = 27 * channels // tiles
    span = -(-width // 128) * 128
    total_width = max(((tiles - 1) * width // 128) * 128 + span + 128, 27 * channels + 128)
    chips = tiles // 2
    hbm = pl.BlockSpec(memory_space=pltpu.HBM)
    vmem = pl.BlockSpec(memory_space=pltpu.VMEM)
    dma = pltpu.SemaphoreType.DMA
    return pl.pallas_call(
        functools.partial(kernel, tiles, chans, width),
        out_shape=(
            jax.ShapeDtypeStruct((outs, VOX), jnp.bfloat16),
            jax.ShapeDtypeStruct((outs, width), jnp.float32),
        ),
        in_specs=[hbm] * 5,
        out_specs=(vmem, vmem),
        scratch_shapes=[
            pltpu.VMEM((1, count), jnp.int32),
            pltpu.VMEM((1, count), jnp.int32),
            pltpu.VMEM((27, outs, channels), jnp.bfloat16),
            pltpu.VMEM((outs, VOX), jnp.bfloat16),
            pltpu.VMEM((tiles, 1, count), jnp.int32),
            pltpu.VMEM((tiles, part, count), jnp.bfloat16),
            pltpu.VMEM((DEPTH * part + 2 * DEPTH, PLANE), jnp.float32),
            pltpu.VMEM((DEPTH, chans, max(part, 16), PLANE), jnp.bfloat16),
            pltpu.VMEM((3 * PLANE, PLANE), jnp.bfloat16),
            pltpu.VMEM((DEPTH, PADDED, 3 * channels), jnp.bfloat16),
            pltpu.VMEM((3 * outs, 9 * channels), jnp.bfloat16),
            pltpu.VMEM((DEPTH + 2, outs, PLANE), jnp.bfloat16),
            pltpu.VMEM((DEPTH, 3 * outs, PLANE), jnp.float32),
            pltpu.VMEM((outs, total_width), jnp.float32),
            pltpu.VMEM((chips, outs, span), jnp.float32),
            pltpu.VMEM((chips, outs, span), jnp.float32),
            pltpu.VMEM((chips, outs, span), jnp.bfloat16),
            pltpu.VMEM((chips, outs, span), jnp.bfloat16),
            dma((5,)),
            dma((chips,)),
            dma((chips,)),
            dma((chips,)),
            dma((chips,)),
            dma((tiles,)),
            dma((tiles,)),
            dma((CHUNKS, chans)),
            dma((CHUNKS, chans)),
            dma((chips,)),
            dma((chips,)),
            dma((chips,)),
            dma((chips,)),
        ],
        compiler_params=pltpu.CompilerParams(
            collective_id=0, has_side_effects=True, vmem_limit_bytes=64 * 1024 * 1024
        ),
    )(
        points,
        dest.reshape(1, count),
        voxel.reshape(1, count),
        jnp.transpose(weight, (1, 0, 2)),
        grad_out,
    )


def solution(mesh):
    placed = (
        P("chan", "tile"),
        P("tile", None),
        P("tile", None),
        P("chan", None, None),
        P("chan", "tile"),
    )
    return jax.shard_map(
        on_device,
        mesh=mesh,
        in_specs=placed,
        out_specs=(P("chan", "tile"), P("chan", "tile")),
        check_vma=False,
    )
```

```python
import functools

import jax
import jax.numpy as jnp
from jax import lax
from jax.experimental import pallas as pl
from jax.experimental.pallas import tpu as pltpu
from jax.sharding import PartitionSpec as P

EDGE = 16
DEPTH = 8
PLANE = EDGE * EDGE
VOX = DEPTH * PLANE
PADDED = PLANE + 2 * EDGE
CHUNKS = 8
LATE = 4
PER_CHUNK = DEPTH // CHUNKS
ROWS_MAJOR = (((1,), (1,)), ((), ()))


def repeat(start, stop, body):
    if stop - start <= 8:
        for step in range(start, stop):
            body(step)
    else:
        lax.fori_loop(start, stop, lambda step, carry: (body(step), carry)[1], 0)


def kernel(
    tiles,
    chans,
    width,
    pts_ref,
    dest_ref,
    voxel_ref,
    weight_ref,
    grad_ref,
    out_ref,
    wgrad_ref,
    dest_here,
    voxel_here,
    weight_here,
    grad_here,
    codes,
    pts_all,
    sums,
    grid,
    shifts,
    moved,
    taps,
    masked,
    partial,
    total,
    handing,
    handed,
    sending,
    received,
    local_sem,
    pts_send,
    pts_recv,
    share_send,
    share_recv,
    code_send,
    code_recv,
    grid_send,
    grid_recv,
    relay_send,
    hand_send,
    hand_recv,
    grad_send,
    grad_recv,
):
    me = lax.axis_index("tile")
    mine = lax.axis_index("chan")
    part = pts_ref.shape[0]
    outs = grad_ref.shape[0]
    channels = part * chans
    span = sending.shape[2]
    chips = tiles // 2
    chip, core = me // 2, lax.rem(me, 2)
    sibling = 2 * chip + 1 - core

    def peer(step):
        return lax.rem(me + step, tiles)

    def giver(step):
        return lax.rem(me + tiles - step, tiles)

    def chip_peer(step):
        return lax.rem(chip + step, chips)

    def chip_giver(step):
        return lax.rem(chip + chips - step, chips)

    def chan_peer(step):
        return lax.rem(mine + step, chans)

    barrier = pltpu.get_barrier_semaphore()

    def greet(step):
        pl.semaphore_signal(barrier, inc=1, device_id={"tile": peer(step)})

    def greet_chan(step):
        pl.semaphore_signal(barrier, inc=1, device_id={"chan": chan_peer(step)})

    def local(place, source, target):
        return pltpu.make_async_copy(source, target, local_sem.at[place])

    fetched = [
        local(0, dest_ref, dest_here),
        local(1, voxel_ref, voxel_here),
        local(2, pts_ref, pts_all.at[me]),
        local(3, weight_ref, weight_here),
        local(4, grad_ref, grad_here),
    ]
    for copy in fetched:
        copy.start()
    repeat(1, tiles, greet)
    repeat(1, chans, greet_chan)
    fetched[0].wait()
    fetched[1].wait()
    codes[me] = dest_here[...] * VOX + voxel_here[...]
    pl.semaphore_wait(barrier, tiles + chans - 2)

    def code_copy(step):
        return pltpu.make_async_remote_copy(
            src_ref=codes.at[me],
            dst_ref=codes.at[me],
            send_sem=code_send.at[step],
            recv_sem=code_recv.at[step],
            device_id={"tile": peer(step)},
        )

    def pts_copy(step):
        return pltpu.make_async_remote_copy(
            src_ref=pts_ref,
            dst_ref=pts_all.at[me],
            send_sem=pts_send.at[step],
            recv_sem=pts_recv.at[step],
            device_id={"tile": 2 * chip_peer(step) + core},
        )

    def share_copy(step):
        origin = 2 * chip_giver(step) + core
        return pltpu.make_async_remote_copy(
            src_ref=pts_all.at[origin],
            dst_ref=pts_all.at[origin],
            send_sem=share_send.at[step],
            recv_sem=share_recv.at[step],
            device_id={"tile": sibling},
        )

    repeat(1, chips, lambda step: pts_copy(step).start())
    repeat(1, tiles, lambda step: code_copy(step).start())
    fetched[2].wait()
    share_copy(0).start()
    fetched[3].wait()

    for a in range(3):
        for tap in range(9):
            taps[a * outs : (a + 1) * outs, tap * channels : (tap + 1) * channels] = weight_here[
                9 * a + tap
            ]
    to = lax.broadcasted_iota(jnp.int32, (PLANE, PLANE), 0)
    source = lax.broadcasted_iota(jnp.int32, (PLANE, PLANE), 1)
    for e in (-1, 0, 1):
        line = (to & (EDGE - 1)) + e
        here = (source == to + e) & (line >= 0) & (line < EDGE)
        shifts[(e + 1) * PLANE : (e + 2) * PLANE, :] = here.astype(jnp.float32).astype(jnp.bfloat16)
    edge = jnp.zeros((EDGE, moved.shape[2]), jnp.bfloat16)
    for plane in range(DEPTH):
        moved[plane, :EDGE, :] = edge
        moved[plane, PADDED - EDGE :, :] = edge
    masked[0] = jnp.zeros((outs, PLANE), jnp.bfloat16)
    masked[DEPTH + 1] = jnp.zeros((outs, PLANE), jnp.bfloat16)

    def add_points(features, code):
        rel = code - me * VOX
        high = rel >> 8
        low = rel & (PLANE - 1)
        count = features.shape[1]
        wide = features.astype(jnp.float32)
        rows = [jnp.where(high == h, wide, 0.0).astype(jnp.bfloat16) for h in range(DEPTH)]
        rank = lax.broadcasted_iota(jnp.int32, (2 * DEPTH, count), 0)
        rows.append((rank == high).astype(jnp.float32).astype(jnp.bfloat16))
        cell = lax.broadcasted_iota(jnp.int32, (PLANE, count), 0)
        onehot = (cell == low).astype(jnp.float32).astype(jnp.bfloat16)
        return lax.dot_general(
            jnp.concatenate(rows, axis=0), onehot, ROWS_MAJOR, preferred_element_type=jnp.float32
        )

    sums[...] = add_points(pts_all[me], codes[me])
    repeat(1, tiles, lambda step: code_copy(step).wait_recv())

    def take_points(origin):
        sums[...] += add_points(pts_all[origin], codes[origin])

    def take_shared(step):
        share_copy(step).wait_recv()
        take_points(2 * chip_giver(step) + 1 - core)

    def take_sent(step):
        pts_copy(step).wait_recv()
        share_copy(step).start()
        take_points(2 * chip_giver(step) + core)

    take_shared(0)
    repeat(1, chips, take_sent)
    repeat(1, chips, take_shared)

    counts = sums[DEPTH * part : DEPTH * part + DEPTH, :]
    floor = jnp.maximum(counts, 1.0)
    occupied = (counts > 0).astype(jnp.float32)
    held = grid.shape[2]

    def grid_copy(chunk, step):
        planes = pl.ds(chunk * PER_CHUNK, PER_CHUNK)
        return pltpu.make_async_remote_copy(
            src_ref=grid.at[planes, mine],
            dst_ref=grid.at[planes, mine],
            send_sem=grid_send.at[chunk, step],
            recv_sem=grid_recv.at[chunk, step],
            device_id={"chan": chan_peer(step)},
        )

    chain = chans == 4
    inner = (mine == 1) | (mine == 2)

    def direct(step, act):
        if chain and step == 1:
            pl.when(mine != 3)(act)
        elif chain and step == 3:
            pl.when(mine != 0)(act)
        else:
            act()

    def relay_copy(chunk):
        planes = pl.ds(chunk * PER_CHUNK, PER_CHUNK)
        origin = lax.rem(mine + 2, chans)
        return pltpu.make_async_remote_copy(
            src_ref=grid.at[planes, origin],
            dst_ref=grid.at[planes, origin],
            send_sem=relay_send.at[chunk],
            recv_sem=grid_recv.at[chunk, jnp.where(mine == 1, 1, 3)],
            device_id={"chan": jnp.where(mine == 1, 0, 3)},
        )

    def pass_on(chunk):
        grid_copy(chunk, 2).wait_recv()

        @pl.when(inner)
        def _():
            relay_copy(chunk).start()

    for chunk in range(CHUNKS):
        for plane in range(chunk * PER_CHUNK, (chunk + 1) * PER_CHUNK):
            mean = sums[plane * part : (plane + 1) * part, :] / floor[plane : plane + 1, :]
            if held > part:
                mean = jnp.concatenate([mean, jnp.zeros((held - part, PLANE), jnp.float32)], axis=0)
            grid[plane, mine] = mean.astype(jnp.bfloat16)
        for step in (2, 1, 3) if chain else range(1, chans):
            direct(step, grid_copy(chunk, step).start)

    fetched[4].wait()
    for plane in range(DEPTH):
        kept = grad_here[:, plane * PLANE : (plane + 1) * PLANE].astype(jnp.float32)
        masked[plane + 1] = (kept * occupied[plane : plane + 1, :]).astype(jnp.bfloat16)

    def columns_of(plane):
        return jnp.concatenate(
            [moved[plane, b * EDGE : b * EDGE + PLANE, :] for b in range(3)], axis=1
        )

    def forward(plane, columns):
        partial[plane] = lax.dot_general(
            taps[...], columns, ROWS_MAJOR, preferred_element_type=jnp.float32
        )

    if chain:
        pass_on(0)
    for chunk in range(CHUNKS):
        if chain and chunk + 1 < CHUNKS:
            pass_on(chunk + 1)
        for step in (1, 3) if chain else range(1, chans):
            grid_copy(chunk, step).wait_recv()
        for plane in range(chunk * PER_CHUNK, (chunk + 1) * PER_CHUNK):
            if held > part:
                lanes = [grid[plane, c].astype(jnp.float32)[:part] for c in range(chans)]
                voxels = jnp.concatenate(lanes, axis=0).astype(jnp.bfloat16)
            else:
                voxels = grid[plane].reshape(channels, PLANE)
            lines = lax.dot_general(
                shifts[...], voxels, ROWS_MAJOR, preferred_element_type=jnp.float32
            ).astype(jnp.bfloat16)
            for e in range(3):
                moved[plane, EDGE : EDGE + PLANE, e * channels : (e + 1) * channels] = lines[
                    e * PLANE : (e + 1) * PLANE, :
                ]
            columns = columns_of(plane)
            if plane < DEPTH - LATE:
                forward(plane, columns)
            cotangents = jnp.concatenate([masked[plane + 2], masked[plane + 1], masked[plane]], axis=0)
            grads = jnp.dot(cotangents, columns, preferred_element_type=jnp.float32)
            for a in range(3):
                place = slice(a * 9 * channels, (a + 1) * 9 * channels)
                piece = grads[a * outs : (a + 1) * outs, :]
                if plane == 0:
                    total[:, place] = piece
                else:
                    total[:, place] += piece
    total[:, 27 * channels :] = jnp.zeros((outs, total.shape[1] - 27 * channels), jnp.float32)

    def block(owner):
        first = owner * width
        base = pl.multiple_of(first // 128 * 128, 128)
        window = total[:, pl.ds(base, span + 128)]
        return pltpu.roll(window, span + 128 - lax.rem(first, 128), 1)[:, :span]

    def hand_copy(step):
        return pltpu.make_async_remote_copy(
            src_ref=handing.at[step],
            dst_ref=handed.at[step],
            send_sem=hand_send.at[step],
            recv_sem=hand_recv.at[step],
            device_id={"tile": sibling},
        )

    def grad_copy(step):
        return pltpu.make_async_remote_copy(
            src_ref=sending.at[step],
            dst_ref=received.at[step],
            send_sem=grad_send.at[step],
            recv_sem=grad_recv.at[step],
            device_id={"tile": 2 * chip_peer(step) + core},
        )

    def hand_grads(step):
        handing[step] = block(2 * chip_peer(step) + 1 - core)
        hand_copy(step).start()

    def send_grads(step):
        own = block(2 * chip_peer(step) + core)
        hand_copy(step).wait_recv()
        sending[step] = (own + handed[step]).astype(jnp.bfloat16)
        grad_copy(step).start()

    repeat(1, chips, hand_grads)
    hand_grads(0)
    repeat(1, chips, send_grads)
    for plane in range(DEPTH - LATE, DEPTH):
        forward(plane, columns_of(plane))

    for plane in range(DEPTH):
        output = partial[plane, outs : 2 * outs, :]
        if plane > 0:
            output = output + partial[plane - 1, :outs, :]
        if plane < DEPTH - 1:
            output = output + partial[plane + 1, 2 * outs :, :]
        out_ref[:, plane * PLANE : (plane + 1) * PLANE] = (
            output * occupied[plane : plane + 1, :]
        ).astype(jnp.bfloat16)

    own_block = block(me)
    hand_copy(0).wait_recv()
    total[:, :span] = own_block + handed[0]

    def take_grads(step):
        grad_copy(step).wait_recv()
        total[:, :span] += received[step].astype(jnp.float32)

    repeat(1, chips, take_grads)
    wgrad_ref[...] = total[:, :width]

    def sent(step):
        pts_copy(step).wait_send()
        grad_copy(step).wait_send()

    def handed_over(step):
        share_copy(step).wait_send()
        hand_copy(step).wait_send()

    repeat(1, tiles, lambda step: code_copy(step).wait_send())
    repeat(1, chips, sent)
    repeat(0, chips, handed_over)
    for chunk in range(CHUNKS):
        for step in range(1, chans):
            direct(step, grid_copy(chunk, step).wait_send)
        if chain:
            pl.when(inner)(relay_copy(chunk).wait_send)


def on_device(points, dest, voxel, weight, grad_out):
    tiles, chans = lax.axis_size("tile"), lax.axis_size("chan")
    part, count = points.shape
    outs = grad_out.shape[0]
    channels = part * chans
    width = 27 * channels // tiles
    span = -(-width // 128) * 128
    total_width = max(((tiles - 1) * width // 128) * 128 + span + 128, 27 * channels + 128)
    chips = tiles // 2
    hbm = pl.BlockSpec(memory_space=pltpu.HBM)
    vmem = pl.BlockSpec(memory_space=pltpu.VMEM)
    dma = pltpu.SemaphoreType.DMA
    return pl.pallas_call(
        functools.partial(kernel, tiles, chans, width),
        out_shape=(
            jax.ShapeDtypeStruct((outs, VOX), jnp.bfloat16),
            jax.ShapeDtypeStruct((outs, width), jnp.float32),
        ),
        in_specs=[hbm] * 5,
        out_specs=(vmem, vmem),
        scratch_shapes=[
            pltpu.VMEM((1, count), jnp.int32),
            pltpu.VMEM((1, count), jnp.int32),
            pltpu.VMEM((27, outs, channels), jnp.bfloat16),
            pltpu.VMEM((outs, VOX), jnp.bfloat16),
            pltpu.VMEM((tiles, 1, count), jnp.int32),
            pltpu.VMEM((tiles, part, count), jnp.bfloat16),
            pltpu.VMEM((DEPTH * part + 2 * DEPTH, PLANE), jnp.float32),
            pltpu.VMEM((DEPTH, chans, max(part, 16), PLANE), jnp.bfloat16),
            pltpu.VMEM((3 * PLANE, PLANE), jnp.bfloat16),
            pltpu.VMEM((DEPTH, PADDED, 3 * channels), jnp.bfloat16),
            pltpu.VMEM((3 * outs, 9 * channels), jnp.bfloat16),
            pltpu.VMEM((DEPTH + 2, outs, PLANE), jnp.bfloat16),
            pltpu.VMEM((DEPTH, 3 * outs, PLANE), jnp.float32),
            pltpu.VMEM((outs, total_width), jnp.float32),
            pltpu.VMEM((chips, outs, span), jnp.float32),
            pltpu.VMEM((chips, outs, span), jnp.float32),
            pltpu.VMEM((chips, outs, span), jnp.bfloat16),
            pltpu.VMEM((chips, outs, span), jnp.bfloat16),
            dma((5,)),
            dma((chips,)),
            dma((chips,)),
            dma((chips,)),
            dma((chips,)),
            dma((tiles,)),
            dma((tiles,)),
            dma((CHUNKS, chans)),
            dma((CHUNKS, chans)),
            dma((CHUNKS,)),
            dma((chips,)),
            dma((chips,)),
            dma((chips,)),
            dma((chips,)),
        ],
        compiler_params=pltpu.CompilerParams(
            collective_id=0, has_side_effects=True, vmem_limit_bytes=64 * 1024 * 1024
        ),
    )(
        points,
        dest.reshape(1, count),
        voxel.reshape(1, count),
        jnp.transpose(weight, (1, 0, 2)),
        grad_out,
    )


def solution(mesh):
    placed = (
        P("chan", "tile"),
        P("tile", None),
        P("tile", None),
        P("chan", None, None),
        P("chan", "tile"),
    )
    return jax.shard_map(
        on_device,
        mesh=mesh,
        in_specs=placed,
        out_specs=(P("chan", "tile"), P("chan", "tile")),
        check_vma=False,
    )
```

```python
import functools

import jax
import jax.numpy as jnp
from jax import lax
from jax.experimental import pallas as pl
from jax.experimental.pallas import tpu as pltpu
from jax.sharding import PartitionSpec as P

EDGE = 16
DEPTH = 8
PLANE = EDGE * EDGE
VOX = DEPTH * PLANE
PADDED = PLANE + 2 * EDGE
CHUNKS = 8
LATE = 4
PER_CHUNK = DEPTH // CHUNKS
ROWS_MAJOR = (((1,), (1,)), ((), ()))


def repeat(start, stop, body):
    if stop - start <= 8:
        for step in range(start, stop):
            body(step)
    else:
        lax.fori_loop(start, stop, lambda step, carry: (body(step), carry)[1], 0)


def kernel(
    tiles,
    chans,
    width,
    pts_ref,
    dest_ref,
    voxel_ref,
    weight_ref,
    grad_ref,
    out_ref,
    wgrad_ref,
    dest_here,
    voxel_here,
    weight_here,
    grad_here,
    codes,
    pts_all,
    sums,
    grid,
    shifts,
    moved,
    stacked,
    taps,
    masked,
    partial,
    total,
    handing,
    handed,
    sending,
    received,
    local_sem,
    pts_send,
    pts_recv,
    share_send,
    share_recv,
    code_send,
    code_recv,
    grid_send,
    grid_recv,
    relay_send,
    hand_send,
    hand_recv,
    grad_send,
    grad_recv,
):
    me = lax.axis_index("tile")
    mine = lax.axis_index("chan")
    part = pts_ref.shape[0]
    outs = grad_ref.shape[0]
    channels = part * chans
    span = sending.shape[2]
    chips = tiles // 2
    chip, core = me // 2, lax.rem(me, 2)
    sibling = 2 * chip + 1 - core

    def peer(step):
        return lax.rem(me + step, tiles)

    def giver(step):
        return lax.rem(me + tiles - step, tiles)

    def chip_peer(step):
        return lax.rem(chip + step, chips)

    def chip_giver(step):
        return lax.rem(chip + chips - step, chips)

    def chan_peer(step):
        return lax.rem(mine + step, chans)

    barrier = pltpu.get_barrier_semaphore()

    def greet(step):
        pl.semaphore_signal(barrier, inc=1, device_id={"tile": peer(step)})

    def greet_chan(step):
        pl.semaphore_signal(barrier, inc=1, device_id={"chan": chan_peer(step)})

    def local(place, source, target):
        return pltpu.make_async_copy(source, target, local_sem.at[place])

    fetched = [
        local(0, dest_ref, dest_here),
        local(1, voxel_ref, voxel_here),
        local(2, pts_ref, pts_all.at[me]),
        local(3, weight_ref, weight_here),
        local(4, grad_ref, grad_here),
    ]
    for copy in fetched:
        copy.start()
    repeat(1, tiles, greet)
    repeat(1, chans, greet_chan)
    fetched[0].wait()
    fetched[1].wait()
    codes[me] = dest_here[...] * VOX + voxel_here[...]
    pl.semaphore_wait(barrier, tiles + chans - 2)

    def code_copy(step):
        return pltpu.make_async_remote_copy(
            src_ref=codes.at[me],
            dst_ref=codes.at[me],
            send_sem=code_send.at[step],
            recv_sem=code_recv.at[step],
            device_id={"tile": peer(step)},
        )

    def pts_copy(step):
        return pltpu.make_async_remote_copy(
            src_ref=pts_ref,
            dst_ref=pts_all.at[me],
            send_sem=pts_send.at[step],
            recv_sem=pts_recv.at[step],
            device_id={"tile": 2 * chip_peer(step) + core},
        )

    def share_copy(step):
        origin = 2 * chip_giver(step) + core
        return pltpu.make_async_remote_copy(
            src_ref=pts_all.at[origin],
            dst_ref=pts_all.at[origin],
            send_sem=share_send.at[step],
            recv_sem=share_recv.at[step],
            device_id={"tile": sibling},
        )

    repeat(1, chips, lambda step: pts_copy(step).start())
    repeat(1, tiles, lambda step: code_copy(step).start())
    fetched[2].wait()
    share_copy(0).start()
    fetched[3].wait()

    for a in range(3):
        for tap in range(9):
            stacked[a * outs : (a + 1) * outs, tap * channels : (tap + 1) * channels] = weight_here[
                9 * a + tap
            ].astype(jnp.float32)
    for tap in range(9):
        place = slice(tap * channels, (tap + 1) * channels)
        taps[place, :] = stacked[:, place].T.astype(jnp.bfloat16)
    to = lax.broadcasted_iota(jnp.int32, (PLANE, PLANE), 0)
    source = lax.broadcasted_iota(jnp.int32, (PLANE, PLANE), 1)
    for e in (-1, 0, 1):
        line = (to & (EDGE - 1)) + e
        here = (source == to + e) & (line >= 0) & (line < EDGE)
        shifts[(e + 1) * PLANE : (e + 2) * PLANE, :] = here.astype(jnp.float32).astype(jnp.bfloat16)
    edge = jnp.zeros((EDGE, moved.shape[2]), jnp.bfloat16)
    for plane in range(DEPTH):
        moved[plane, :EDGE, :] = edge
        moved[plane, PADDED - EDGE :, :] = edge
    masked[0] = jnp.zeros((outs, PLANE), jnp.bfloat16)
    masked[DEPTH + 1] = jnp.zeros((outs, PLANE), jnp.bfloat16)

    def add_points(features, code):
        rel = code - me * VOX
        high = rel >> 8
        low = rel & (PLANE - 1)
        count = features.shape[1]
        wide = features.astype(jnp.float32)
        rows = [jnp.where(high == h, wide, 0.0).astype(jnp.bfloat16) for h in range(DEPTH)]
        rank = lax.broadcasted_iota(jnp.int32, (2 * DEPTH, count), 0)
        rows.append((rank == high).astype(jnp.float32).astype(jnp.bfloat16))
        cell = lax.broadcasted_iota(jnp.int32, (PLANE, count), 0)
        onehot = (cell == low).astype(jnp.float32).astype(jnp.bfloat16)
        return lax.dot_general(
            jnp.concatenate(rows, axis=0), onehot, ROWS_MAJOR, preferred_element_type=jnp.float32
        )

    sums[...] = add_points(pts_all[me], codes[me])
    repeat(1, tiles, lambda step: code_copy(step).wait_recv())

    def take_points(origin):
        sums[...] += add_points(pts_all[origin], codes[origin])

    def take_shared(step):
        share_copy(step).wait_recv()
        take_points(2 * chip_giver(step) + 1 - core)

    def take_sent(step):
        pts_copy(step).wait_recv()
        share_copy(step).start()
        take_points(2 * chip_giver(step) + core)

    take_shared(0)
    repeat(1, chips, take_sent)
    repeat(1, chips, take_shared)

    counts = sums[DEPTH * part : DEPTH * part + DEPTH, :]
    floor = jnp.maximum(counts, 1.0)
    occupied = (counts > 0).astype(jnp.float32)
    held = grid.shape[2]

    def grid_copy(chunk, step):
        planes = pl.ds(chunk * PER_CHUNK, PER_CHUNK)
        return pltpu.make_async_remote_copy(
            src_ref=grid.at[planes, mine],
            dst_ref=grid.at[planes, mine],
            send_sem=grid_send.at[chunk, step],
            recv_sem=grid_recv.at[chunk, step],
            device_id={"chan": chan_peer(step)},
        )

    chain = chans == 4
    inner = (mine == 1) | (mine == 2)

    def direct(step, act):
        if chain and step == 1:
            pl.when(mine != 3)(act)
        elif chain and step == 3:
            pl.when(mine != 0)(act)
        else:
            act()

    def relay_copy(chunk):
        planes = pl.ds(chunk * PER_CHUNK, PER_CHUNK)
        origin = lax.rem(mine + 2, chans)
        return pltpu.make_async_remote_copy(
            src_ref=grid.at[planes, origin],
            dst_ref=grid.at[planes, origin],
            send_sem=relay_send.at[chunk],
            recv_sem=grid_recv.at[chunk, jnp.where(mine == 1, 1, 3)],
            device_id={"chan": jnp.where(mine == 1, 0, 3)},
        )

    def pass_on(chunk):
        grid_copy(chunk, 2).wait_recv()

        @pl.when(inner)
        def _():
            relay_copy(chunk).start()

    for chunk in range(CHUNKS):
        for plane in range(chunk * PER_CHUNK, (chunk + 1) * PER_CHUNK):
            mean = sums[plane * part : (plane + 1) * part, :] / floor[plane : plane + 1, :]
            if held > part:
                mean = jnp.concatenate([mean, jnp.zeros((held - part, PLANE), jnp.float32)], axis=0)
            grid[plane, mine] = mean.astype(jnp.bfloat16)
        for step in (2, 1, 3) if chain else range(1, chans):
            direct(step, grid_copy(chunk, step).start)

    fetched[4].wait()
    for plane in range(DEPTH):
        kept = grad_here[:, plane * PLANE : (plane + 1) * PLANE].astype(jnp.float32)
        masked[plane + 1] = (kept * occupied[plane : plane + 1, :]).astype(jnp.bfloat16)

    def columns_of(plane):
        return jnp.concatenate(
            [moved[plane, b * EDGE : b * EDGE + PLANE, :] for b in range(3)], axis=1
        )

    def forward(plane, columns):
        partial[plane] = jnp.dot(columns, taps[...], preferred_element_type=jnp.float32).T

    if chain:
        pass_on(0)
    for chunk in range(CHUNKS):
        if chain and chunk + 1 < CHUNKS:
            pass_on(chunk + 1)
        for step in (1, 3) if chain else range(1, chans):
            grid_copy(chunk, step).wait_recv()
        for plane in range(chunk * PER_CHUNK, (chunk + 1) * PER_CHUNK):
            if held > part:
                lanes = [grid[plane, c].astype(jnp.float32)[:part] for c in range(chans)]
                voxels = jnp.concatenate(lanes, axis=0).astype(jnp.bfloat16)
            else:
                voxels = grid[plane].reshape(channels, PLANE)
            lines = lax.dot_general(
                shifts[...], voxels, ROWS_MAJOR, preferred_element_type=jnp.float32
            ).astype(jnp.bfloat16)
            for e in range(3):
                moved[plane, EDGE : EDGE + PLANE, e * channels : (e + 1) * channels] = lines[
                    e * PLANE : (e + 1) * PLANE, :
                ]
            columns = columns_of(plane)
            if plane < DEPTH - LATE:
                forward(plane, columns)
            cotangents = jnp.concatenate([masked[plane + 2], masked[plane + 1], masked[plane]], axis=0)
            grads = jnp.dot(cotangents, columns, preferred_element_type=jnp.float32)
            for a in range(3):
                place = slice(a * 9 * channels, (a + 1) * 9 * channels)
                piece = grads[a * outs : (a + 1) * outs, :]
                if plane == 0:
                    total[:, place] = piece
                else:
                    total[:, place] += piece
    total[:, 27 * channels :] = jnp.zeros((outs, total.shape[1] - 27 * channels), jnp.float32)

    def block(owner):
        first = owner * width
        base = pl.multiple_of(first // 128 * 128, 128)
        window = total[:, pl.ds(base, span + 128)]
        return pltpu.roll(window, span + 128 - lax.rem(first, 128), 1)[:, :span]

    def hand_copy(step):
        return pltpu.make_async_remote_copy(
            src_ref=handing.at[step],
            dst_ref=handed.at[step],
            send_sem=hand_send.at[step],
            recv_sem=hand_recv.at[step],
            device_id={"tile": sibling},
        )

    def grad_copy(step):
        return pltpu.make_async_remote_copy(
            src_ref=sending.at[step],
            dst_ref=received.at[step],
            send_sem=grad_send.at[step],
            recv_sem=grad_recv.at[step],
            device_id={"tile": 2 * chip_peer(step) + core},
        )

    def hand_grads(step):
        handing[step] = block(2 * chip_peer(step) + 1 - core)
        hand_copy(step).start()

    def send_grads(step):
        own = block(2 * chip_peer(step) + core)
        hand_copy(step).wait_recv()
        sending[step] = (own + handed[step]).astype(jnp.bfloat16)
        grad_copy(step).start()

    repeat(1, chips, hand_grads)
    hand_grads(0)
    repeat(1, chips, send_grads)
    for plane in range(DEPTH - LATE, DEPTH):
        forward(plane, columns_of(plane))

    for plane in range(DEPTH):
        output = partial[plane, outs : 2 * outs, :]
        if plane > 0:
            output = output + partial[plane - 1, :outs, :]
        if plane < DEPTH - 1:
            output = output + partial[plane + 1, 2 * outs :, :]
        out_ref[:, plane * PLANE : (plane + 1) * PLANE] = (
            output * occupied[plane : plane + 1, :]
        ).astype(jnp.bfloat16)

    own_block = block(me)
    hand_copy(0).wait_recv()
    total[:, :span] = own_block + handed[0]

    def take_grads(step):
        grad_copy(step).wait_recv()
        total[:, :span] += received[step].astype(jnp.float32)

    repeat(1, chips, take_grads)
    wgrad_ref[...] = total[:, :width]

    def sent(step):
        pts_copy(step).wait_send()
        grad_copy(step).wait_send()

    def handed_over(step):
        share_copy(step).wait_send()
        hand_copy(step).wait_send()

    repeat(1, tiles, lambda step: code_copy(step).wait_send())
    repeat(1, chips, sent)
    repeat(0, chips, handed_over)
    for chunk in range(CHUNKS):
        for step in range(1, chans):
            direct(step, grid_copy(chunk, step).wait_send)
        if chain:
            pl.when(inner)(relay_copy(chunk).wait_send)


def on_device(points, dest, voxel, weight, grad_out):
    tiles, chans = lax.axis_size("tile"), lax.axis_size("chan")
    part, count = points.shape
    outs = grad_out.shape[0]
    channels = part * chans
    width = 27 * channels // tiles
    span = -(-width // 128) * 128
    total_width = max(((tiles - 1) * width // 128) * 128 + span + 128, 27 * channels + 128)
    chips = tiles // 2
    hbm = pl.BlockSpec(memory_space=pltpu.HBM)
    vmem = pl.BlockSpec(memory_space=pltpu.VMEM)
    dma = pltpu.SemaphoreType.DMA
    return pl.pallas_call(
        functools.partial(kernel, tiles, chans, width),
        out_shape=(
            jax.ShapeDtypeStruct((outs, VOX), jnp.bfloat16),
            jax.ShapeDtypeStruct((outs, width), jnp.float32),
        ),
        in_specs=[hbm] * 5,
        out_specs=(vmem, vmem),
        scratch_shapes=[
            pltpu.VMEM((1, count), jnp.int32),
            pltpu.VMEM((1, count), jnp.int32),
            pltpu.VMEM((27, outs, channels), jnp.bfloat16),
            pltpu.VMEM((outs, VOX), jnp.bfloat16),
            pltpu.VMEM((tiles, 1, count), jnp.int32),
            pltpu.VMEM((tiles, part, count), jnp.bfloat16),
            pltpu.VMEM((DEPTH * part + 2 * DEPTH, PLANE), jnp.float32),
            pltpu.VMEM((DEPTH, chans, max(part, 16), PLANE), jnp.bfloat16),
            pltpu.VMEM((3 * PLANE, PLANE), jnp.bfloat16),
            pltpu.VMEM((DEPTH, PADDED, 3 * channels), jnp.bfloat16),
            pltpu.VMEM((3 * outs, 9 * channels), jnp.float32),
            pltpu.VMEM((9 * channels, 3 * outs), jnp.bfloat16),
            pltpu.VMEM((DEPTH + 2, outs, PLANE), jnp.bfloat16),
            pltpu.VMEM((DEPTH, 3 * outs, PLANE), jnp.float32),
            pltpu.VMEM((outs, total_width), jnp.float32),
            pltpu.VMEM((chips, outs, span), jnp.float32),
            pltpu.VMEM((chips, outs, span), jnp.float32),
            pltpu.VMEM((chips, outs, span), jnp.bfloat16),
            pltpu.VMEM((chips, outs, span), jnp.bfloat16),
            dma((5,)),
            dma((chips,)),
            dma((chips,)),
            dma((chips,)),
            dma((chips,)),
            dma((tiles,)),
            dma((tiles,)),
            dma((CHUNKS, chans)),
            dma((CHUNKS, chans)),
            dma((CHUNKS,)),
            dma((chips,)),
            dma((chips,)),
            dma((chips,)),
            dma((chips,)),
        ],
        compiler_params=pltpu.CompilerParams(
            collective_id=0, has_side_effects=True, vmem_limit_bytes=48 * 1024 * 1024
        ),
    )(
        *(
            pltpu.with_memory_space_constraint(operand, pltpu.HBM)
            for operand in (
                points,
                dest.reshape(1, count),
                voxel.reshape(1, count),
                jnp.transpose(weight, (1, 0, 2)),
                grad_out,
            )
        )
    )


def solution(mesh):
    placed = (
        P("chan", "tile"),
        P("tile", None),
        P("tile", None),
        P("chan", None, None),
        P("chan", "tile"),
    )
    return jax.shard_map(
        on_device,
        mesh=mesh,
        in_specs=placed,
        out_specs=(P("chan", "tile"), P("chan", "tile")),
        check_vma=False,
    )
```

```python
import functools

import jax
import jax.numpy as jnp
from jax import lax
from jax.experimental import pallas as pl
from jax.experimental.pallas import tpu as pltpu
from jax.sharding import PartitionSpec as P

EDGE = 16
DEPTH = 8
PLANE = EDGE * EDGE
VOX = DEPTH * PLANE
PADDED = PLANE + 2 * EDGE
CHUNKS = 8
LATE = 6
PER_CHUNK = DEPTH // CHUNKS
ROWS_MAJOR = (((1,), (1,)), ((), ()))


def repeat(start, stop, body):
    if stop - start <= 8:
        for step in range(start, stop):
            body(step)
    else:
        lax.fori_loop(start, stop, lambda step, carry: (body(step), carry)[1], 0)


def kernel(
    tiles,
    chans,
    width,
    pts_ref,
    dest_ref,
    voxel_ref,
    weight_ref,
    grad_ref,
    out_ref,
    wgrad_ref,
    dest_here,
    voxel_here,
    weight_here,
    grad_here,
    codes,
    pts_all,
    sums,
    grid,
    shifts,
    moved,
    stacked,
    taps,
    masked,
    partial,
    total,
    handing,
    handed,
    sending,
    received,
    local_sem,
    pts_send,
    pts_recv,
    share_send,
    share_recv,
    code_send,
    code_recv,
    grid_send,
    grid_recv,
    relay_send,
    hand_send,
    hand_recv,
    grad_send,
    grad_recv,
):
    me = lax.axis_index("tile")
    mine = lax.axis_index("chan")
    part = pts_ref.shape[0]
    outs = grad_ref.shape[0]
    channels = part * chans
    span = sending.shape[2]
    chips = tiles // 2
    chip, core = me // 2, lax.rem(me, 2)
    sibling = 2 * chip + 1 - core

    def peer(step):
        return lax.rem(me + step, tiles)

    def giver(step):
        return lax.rem(me + tiles - step, tiles)

    def chip_peer(step):
        return lax.rem(chip + step, chips)

    def chip_giver(step):
        return lax.rem(chip + chips - step, chips)

    def chan_peer(step):
        return lax.rem(mine + step, chans)

    barrier = pltpu.get_barrier_semaphore()

    def greet(step):
        pl.semaphore_signal(barrier, inc=1, device_id={"tile": peer(step)})

    def greet_chan(step):
        pl.semaphore_signal(barrier, inc=1, device_id={"chan": chan_peer(step)})

    def local(place, source, target):
        return pltpu.make_async_copy(source, target, local_sem.at[place])

    fetched = [
        local(0, dest_ref, dest_here),
        local(1, voxel_ref, voxel_here),
        local(2, pts_ref, pts_all.at[me]),
        local(3, weight_ref, weight_here),
        local(4, grad_ref, grad_here),
    ]
    for copy in fetched:
        copy.start()
    repeat(1, tiles, greet)
    repeat(1, chans, greet_chan)
    fetched[0].wait()
    fetched[1].wait()
    codes[me] = dest_here[...] * VOX + voxel_here[...]
    pl.semaphore_wait(barrier, tiles + chans - 2)

    def code_copy(step):
        return pltpu.make_async_remote_copy(
            src_ref=codes.at[me],
            dst_ref=codes.at[me],
            send_sem=code_send.at[step],
            recv_sem=code_recv.at[step],
            device_id={"tile": peer(step)},
        )

    def pts_copy(step):
        return pltpu.make_async_remote_copy(
            src_ref=pts_ref,
            dst_ref=pts_all.at[me],
            send_sem=pts_send.at[step],
            recv_sem=pts_recv.at[step],
            device_id={"tile": 2 * chip_peer(step) + core},
        )

    def share_copy(step):
        origin = 2 * chip_giver(step) + core
        return pltpu.make_async_remote_copy(
            src_ref=pts_all.at[origin],
            dst_ref=pts_all.at[origin],
            send_sem=share_send.at[step],
            recv_sem=share_recv.at[step],
            device_id={"tile": sibling},
        )

    repeat(1, chips, lambda step: pts_copy(step).start())
    repeat(1, tiles, lambda step: code_copy(step).start())
    fetched[2].wait()
    share_copy(0).start()

    to = lax.broadcasted_iota(jnp.int32, (PLANE, PLANE), 0)
    source = lax.broadcasted_iota(jnp.int32, (PLANE, PLANE), 1)
    for e in (-1, 0, 1):
        line = (to & (EDGE - 1)) + e
        here = (source == to + e) & (line >= 0) & (line < EDGE)
        shifts[(e + 1) * PLANE : (e + 2) * PLANE, :] = here.astype(jnp.float32).astype(jnp.bfloat16)
    edge = jnp.zeros((EDGE, moved.shape[2]), jnp.bfloat16)
    for plane in range(DEPTH):
        moved[plane, :EDGE, :] = edge
        moved[plane, PADDED - EDGE :, :] = edge
    masked[0] = jnp.zeros((outs, PLANE), jnp.bfloat16)
    masked[DEPTH + 1] = jnp.zeros((outs, PLANE), jnp.bfloat16)

    def add_points(features, code):
        rel = code - me * VOX
        high = rel >> 8
        low = rel & (PLANE - 1)
        count = features.shape[1]
        wide = features.astype(jnp.float32)
        rows = [jnp.where(high == h, wide, 0.0).astype(jnp.bfloat16) for h in range(DEPTH)]
        rank = lax.broadcasted_iota(jnp.int32, (2 * DEPTH, count), 0)
        rows.append((rank == high).astype(jnp.float32).astype(jnp.bfloat16))
        cell = lax.broadcasted_iota(jnp.int32, (PLANE, count), 0)
        onehot = (cell == low).astype(jnp.float32).astype(jnp.bfloat16)
        return lax.dot_general(
            jnp.concatenate(rows, axis=0), onehot, ROWS_MAJOR, preferred_element_type=jnp.float32
        )

    sums[...] = add_points(pts_all[me], codes[me])
    repeat(1, tiles, lambda step: code_copy(step).wait_recv())

    def take_points(origin):
        sums[...] += add_points(pts_all[origin], codes[origin])

    def take_shared(step):
        share_copy(step).wait_recv()
        take_points(2 * chip_giver(step) + 1 - core)

    def take_sent(step):
        pts_copy(step).wait_recv()
        share_copy(step).start()
        take_points(2 * chip_giver(step) + core)

    take_shared(0)
    repeat(1, chips, take_sent)
    repeat(1, chips, take_shared)

    counts = sums[DEPTH * part : DEPTH * part + DEPTH, :]
    floor = jnp.maximum(counts, 1.0)
    occupied = (counts > 0).astype(jnp.float32)
    held = grid.shape[2]

    def grid_copy(chunk, step):
        planes = pl.ds(chunk * PER_CHUNK, PER_CHUNK)
        return pltpu.make_async_remote_copy(
            src_ref=grid.at[planes, mine],
            dst_ref=grid.at[planes, mine],
            send_sem=grid_send.at[chunk, step],
            recv_sem=grid_recv.at[chunk, step],
            device_id={"chan": chan_peer(step)},
        )

    chain = chans == 4
    inner = (mine == 1) | (mine == 2)

    def direct(step, act):
        if chain and step == 1:
            pl.when(mine != 3)(act)
        elif chain and step == 3:
            pl.when(mine != 0)(act)
        else:
            act()

    def relay_copy(chunk):
        planes = pl.ds(chunk * PER_CHUNK, PER_CHUNK)
        origin = lax.rem(mine + 2, chans)
        return pltpu.make_async_remote_copy(
            src_ref=grid.at[planes, origin],
            dst_ref=grid.at[planes, origin],
            send_sem=relay_send.at[chunk],
            recv_sem=grid_recv.at[chunk, jnp.where(mine == 1, 1, 3)],
            device_id={"chan": jnp.where(mine == 1, 0, 3)},
        )

    def pass_on(chunk):
        @pl.when(inner)
        def _():
            grid_copy(chunk, 2).wait_recv()
            relay_copy(chunk).start()

    for chunk in range(CHUNKS):
        for plane in range(chunk * PER_CHUNK, (chunk + 1) * PER_CHUNK):
            mean = sums[plane * part : (plane + 1) * part, :] / floor[plane : plane + 1, :]
            if held > part:
                mean = jnp.concatenate([mean, jnp.zeros((held - part, PLANE), jnp.float32)], axis=0)
            grid[plane, mine] = mean.astype(jnp.bfloat16)
        for step in (2, 1, 3) if chain else range(1, chans):
            direct(step, grid_copy(chunk, step).start)

    fetched[3].wait()
    for a in range(3):
        for tap in range(9):
            stacked[a * outs : (a + 1) * outs, tap * channels : (tap + 1) * channels] = weight_here[
                9 * a + tap
            ].astype(jnp.float32)
    for tap in range(9):
        place = slice(tap * channels, (tap + 1) * channels)
        taps[place, :] = stacked[:, place].T.astype(jnp.bfloat16)
    fetched[4].wait()
    for plane in range(DEPTH):
        kept = grad_here[:, plane * PLANE : (plane + 1) * PLANE].astype(jnp.float32)
        masked[plane + 1] = (kept * occupied[plane : plane + 1, :]).astype(jnp.bfloat16)

    def columns_of(plane):
        return jnp.concatenate(
            [moved[plane, b * EDGE : b * EDGE + PLANE, :] for b in range(3)], axis=1
        )

    def forward(plane, columns):
        partial[plane] = jnp.dot(columns, taps[...], preferred_element_type=jnp.float32).T

    if chain:
        pass_on(0)
    for chunk in range(CHUNKS):
        if chain and chunk + 1 < CHUNKS:
            pass_on(chunk + 1)
        for step in (1, 3) if chain else range(1, chans):
            grid_copy(chunk, step).wait_recv()
        if chain:
            pl.when(jnp.logical_not(inner))(grid_copy(chunk, 2).wait_recv)
        for plane in range(chunk * PER_CHUNK, (chunk + 1) * PER_CHUNK):
            if held > part:
                lanes = [grid[plane, c].astype(jnp.float32)[:part] for c in range(chans)]
                voxels = jnp.concatenate(lanes, axis=0).astype(jnp.bfloat16)
            else:
                voxels = grid[plane].reshape(channels, PLANE)
            lines = lax.dot_general(
                shifts[...], voxels, ROWS_MAJOR, preferred_element_type=jnp.float32
            ).astype(jnp.bfloat16)
            for e in range(3):
                moved[plane, EDGE : EDGE + PLANE, e * channels : (e + 1) * channels] = lines[
                    e * PLANE : (e + 1) * PLANE, :
                ]
            columns = columns_of(plane)
            if plane < DEPTH - LATE:
                forward(plane, columns)
            cotangents = jnp.concatenate([masked[plane + 2], masked[plane + 1], masked[plane]], axis=0)
            grads = jnp.dot(cotangents, columns, preferred_element_type=jnp.float32)
            for a in range(3):
                place = slice(a * 9 * channels, (a + 1) * 9 * channels)
                piece = grads[a * outs : (a + 1) * outs, :]
                if plane == 0:
                    total[:, place] = piece
                else:
                    total[:, place] += piece
    total[:, 27 * channels :] = jnp.zeros((outs, total.shape[1] - 27 * channels), jnp.float32)

    def block(owner):
        first = owner * width
        base = pl.multiple_of(first // 128 * 128, 128)
        window = total[:, pl.ds(base, span + 128)]
        return pltpu.roll(window, span + 128 - lax.rem(first, 128), 1)[:, :span]

    def hand_copy(step):
        return pltpu.make_async_remote_copy(
            src_ref=handing.at[step],
            dst_ref=handed.at[step],
            send_sem=hand_send.at[step],
            recv_sem=hand_recv.at[step],
            device_id={"tile": sibling},
        )

    def grad_copy(step):
        return pltpu.make_async_remote_copy(
            src_ref=sending.at[step],
            dst_ref=received.at[step],
            send_sem=grad_send.at[step],
            recv_sem=grad_recv.at[step],
            device_id={"tile": 2 * chip_peer(step) + core},
        )

    def hand_grads(step):
        handing[step] = block(2 * chip_peer(step) + 1 - core)
        hand_copy(step).start()

    def send_grads(step):
        own = block(2 * chip_peer(step) + core)
        hand_copy(step).wait_recv()
        sending[step] = (own + handed[step]).astype(jnp.bfloat16)
        grad_copy(step).start()

    repeat(1, chips, hand_grads)
    hand_grads(0)
    repeat(1, chips, send_grads)
    for plane in range(DEPTH - LATE, DEPTH):
        forward(plane, columns_of(plane))

    for plane in range(DEPTH):
        output = partial[plane, outs : 2 * outs, :]
        if plane > 0:
            output = output + partial[plane - 1, :outs, :]
        if plane < DEPTH - 1:
            output = output + partial[plane + 1, 2 * outs :, :]
        out_ref[:, plane * PLANE : (plane + 1) * PLANE] = (
            output * occupied[plane : plane + 1, :]
        ).astype(jnp.bfloat16)

    own_block = block(me)
    hand_copy(0).wait_recv()
    total[:, :span] = own_block + handed[0]

    def take_grads(step):
        grad_copy(step).wait_recv()
        total[:, :span] += received[step].astype(jnp.float32)

    repeat(1, chips, take_grads)
    wgrad_ref[...] = total[:, :width]

    def sent(step):
        pts_copy(step).wait_send()
        grad_copy(step).wait_send()

    def handed_over(step):
        share_copy(step).wait_send()
        hand_copy(step).wait_send()

    repeat(1, tiles, lambda step: code_copy(step).wait_send())
    repeat(1, chips, sent)
    repeat(0, chips, handed_over)
    for chunk in range(CHUNKS):
        for step in range(1, chans):
            direct(step, grid_copy(chunk, step).wait_send)
        if chain:
            pl.when(inner)(relay_copy(chunk).wait_send)


def on_device(points, dest, voxel, weight, grad_out):
    tiles, chans = lax.axis_size("tile"), lax.axis_size("chan")
    part, count = points.shape
    outs = grad_out.shape[0]
    channels = part * chans
    width = 27 * channels // tiles
    span = -(-width // 128) * 128
    total_width = max(((tiles - 1) * width // 128) * 128 + span + 128, 27 * channels + 128)
    chips = tiles // 2
    hbm = pl.BlockSpec(memory_space=pltpu.HBM)
    vmem = pl.BlockSpec(memory_space=pltpu.VMEM)
    dma = pltpu.SemaphoreType.DMA
    return pl.pallas_call(
        functools.partial(kernel, tiles, chans, width),
        out_shape=(
            jax.ShapeDtypeStruct((outs, VOX), jnp.bfloat16),
            jax.ShapeDtypeStruct((outs, width), jnp.float32),
        ),
        in_specs=[hbm] * 5,
        out_specs=(vmem, vmem),
        scratch_shapes=[
            pltpu.VMEM((1, count), jnp.int32),
            pltpu.VMEM((1, count), jnp.int32),
            pltpu.VMEM((27, outs, channels), jnp.bfloat16),
            pltpu.VMEM((outs, VOX), jnp.bfloat16),
            pltpu.VMEM((tiles, 1, count), jnp.int32),
            pltpu.VMEM((tiles, part, count), jnp.bfloat16),
            pltpu.VMEM((DEPTH * part + 2 * DEPTH, PLANE), jnp.float32),
            pltpu.VMEM((DEPTH, chans, max(part, 16), PLANE), jnp.bfloat16),
            pltpu.VMEM((3 * PLANE, PLANE), jnp.bfloat16),
            pltpu.VMEM((DEPTH, PADDED, 3 * channels), jnp.bfloat16),
            pltpu.VMEM((3 * outs, 9 * channels), jnp.float32),
            pltpu.VMEM((9 * channels, 3 * outs), jnp.bfloat16),
            pltpu.VMEM((DEPTH + 2, outs, PLANE), jnp.bfloat16),
            pltpu.VMEM((DEPTH, 3 * outs, PLANE), jnp.float32),
            pltpu.VMEM((outs, total_width), jnp.float32),
            pltpu.VMEM((chips, outs, span), jnp.float32),
            pltpu.VMEM((chips, outs, span), jnp.float32),
            pltpu.VMEM((chips, outs, span), jnp.bfloat16),
            pltpu.VMEM((chips, outs, span), jnp.bfloat16),
            dma((5,)),
            dma((chips,)),
            dma((chips,)),
            dma((chips,)),
            dma((chips,)),
            dma((tiles,)),
            dma((tiles,)),
            dma((CHUNKS, chans)),
            dma((CHUNKS, chans)),
            dma((CHUNKS,)),
            dma((chips,)),
            dma((chips,)),
            dma((chips,)),
            dma((chips,)),
        ],
        compiler_params=pltpu.CompilerParams(
            collective_id=0, has_side_effects=True, vmem_limit_bytes=48 * 1024 * 1024
        ),
    )(
        *(
            pltpu.with_memory_space_constraint(operand, pltpu.HBM)
            for operand in (
                points,
                dest.reshape(1, count),
                voxel.reshape(1, count),
                jnp.transpose(weight, (1, 0, 2)),
                grad_out,
            )
        )
    )


def solution(mesh):
    placed = (
        P("chan", "tile"),
        P("tile", None),
        P("tile", None),
        P("chan", None, None),
        P("chan", "tile"),
    )
    return jax.shard_map(
        on_device,
        mesh=mesh,
        in_specs=placed,
        out_specs=(P("chan", "tile"), P("chan", "tile")),
        check_vma=False,
    )
```

```python
import functools

import jax
import jax.numpy as jnp
from jax import lax
from jax.experimental import pallas as pl
from jax.experimental.pallas import tpu as pltpu
from jax.sharding import PartitionSpec as P

EDGE = 16
DEPTH = 8
PLANE = EDGE * EDGE
VOX = DEPTH * PLANE
PADDED = PLANE + 2 * EDGE
CHUNKS = 8
LATE = 6
PER_CHUNK = DEPTH // CHUNKS
ROWS_MAJOR = (((1,), (1,)), ((), ()))


def repeat(start, stop, body):
    if stop - start <= 8:
        for step in range(start, stop):
            body(step)
    else:
        lax.fori_loop(start, stop, lambda step, carry: (body(step), carry)[1], 0)


def kernel(
    tiles,
    chans,
    width,
    pts_ref,
    dest_ref,
    voxel_ref,
    weight_ref,
    grad_ref,
    out_ref,
    wgrad_ref,
    dest_here,
    voxel_here,
    weight_here,
    grad_here,
    codes,
    pts_all,
    sums,
    grid,
    shifts,
    moved,
    stacked,
    taps,
    masked,
    partial,
    total,
    blocks,
    handing,
    handed,
    sending,
    received,
    local_sem,
    pts_send,
    pts_recv,
    share_send,
    share_recv,
    code_send,
    code_recv,
    grid_send,
    grid_recv,
    relay_send,
    hand_send,
    hand_recv,
    grad_send,
    grad_recv,
):
    me = lax.axis_index("tile")
    mine = lax.axis_index("chan")
    part = pts_ref.shape[0]
    outs = grad_ref.shape[0]
    channels = part * chans
    span = sending.shape[2]
    chips = tiles // 2
    chip, core = me // 2, lax.rem(me, 2)
    sibling = 2 * chip + 1 - core

    def peer(step):
        return lax.rem(me + step, tiles)

    def giver(step):
        return lax.rem(me + tiles - step, tiles)

    def chip_peer(step):
        return lax.rem(chip + step, chips)

    def chip_giver(step):
        return lax.rem(chip + chips - step, chips)

    def chan_peer(step):
        return lax.rem(mine + step, chans)

    barrier = pltpu.get_barrier_semaphore()

    def greet(step):
        pl.semaphore_signal(barrier, inc=1, device_id={"tile": peer(step)})

    def greet_chan(step):
        pl.semaphore_signal(barrier, inc=1, device_id={"chan": chan_peer(step)})

    def local(place, source, target):
        return pltpu.make_async_copy(source, target, local_sem.at[place])

    fetched = [
        local(0, dest_ref, dest_here),
        local(1, voxel_ref, voxel_here),
        local(2, pts_ref, pts_all.at[me]),
        local(3, weight_ref, weight_here),
        local(4, grad_ref, grad_here),
    ]
    for copy in fetched:
        copy.start()
    repeat(1, tiles, greet)
    repeat(1, chans, greet_chan)
    fetched[0].wait()
    fetched[1].wait()
    codes[me] = dest_here[...] * VOX + voxel_here[...]
    pl.semaphore_wait(barrier, tiles + chans - 2)

    def code_copy(step):
        return pltpu.make_async_remote_copy(
            src_ref=codes.at[me],
            dst_ref=codes.at[me],
            send_sem=code_send.at[step],
            recv_sem=code_recv.at[step],
            device_id={"tile": peer(step)},
        )

    def pts_copy(step):
        return pltpu.make_async_remote_copy(
            src_ref=pts_ref,
            dst_ref=pts_all.at[me],
            send_sem=pts_send.at[step],
            recv_sem=pts_recv.at[step],
            device_id={"tile": 2 * chip_peer(step) + core},
        )

    def share_copy(step):
        origin = 2 * chip_giver(step) + core
        return pltpu.make_async_remote_copy(
            src_ref=pts_all.at[origin],
            dst_ref=pts_all.at[origin],
            send_sem=share_send.at[step],
            recv_sem=share_recv.at[step],
            device_id={"tile": sibling},
        )

    repeat(1, chips, lambda step: pts_copy(step).start())
    repeat(1, tiles, lambda step: code_copy(step).start())
    fetched[2].wait()
    share_copy(0).start()

    to = lax.broadcasted_iota(jnp.int32, (PLANE, PLANE), 0)
    source = lax.broadcasted_iota(jnp.int32, (PLANE, PLANE), 1)
    for e in (-1, 0, 1):
        line = (to & (EDGE - 1)) + e
        here = (source == to + e) & (line >= 0) & (line < EDGE)
        shifts[(e + 1) * PLANE : (e + 2) * PLANE, :] = here.astype(jnp.float32).astype(jnp.bfloat16)
    edge = jnp.zeros((EDGE, moved.shape[2]), jnp.bfloat16)
    for plane in range(DEPTH):
        moved[plane, :EDGE, :] = edge
        moved[plane, PADDED - EDGE :, :] = edge
    masked[0] = jnp.zeros((outs, PLANE), jnp.bfloat16)
    masked[DEPTH + 1] = jnp.zeros((outs, PLANE), jnp.bfloat16)

    def add_points(features, code):
        rel = code - me * VOX
        high = rel >> 8
        low = rel & (PLANE - 1)
        count = features.shape[1]
        wide = features.astype(jnp.float32)
        rows = [jnp.where(high == h, wide, 0.0).astype(jnp.bfloat16) for h in range(DEPTH)]
        rank = lax.broadcasted_iota(jnp.int32, (2 * DEPTH, count), 0)
        rows.append((rank == high).astype(jnp.float32).astype(jnp.bfloat16))
        cell = lax.broadcasted_iota(jnp.int32, (PLANE, count), 0)
        onehot = (cell == low).astype(jnp.float32).astype(jnp.bfloat16)
        return lax.dot_general(
            jnp.concatenate(rows, axis=0), onehot, ROWS_MAJOR, preferred_element_type=jnp.float32
        )

    sums[...] = add_points(pts_all[me], codes[me])
    repeat(1, tiles, lambda step: code_copy(step).wait_recv())

    def take_points(origin):
        sums[...] += add_points(pts_all[origin], codes[origin])

    def take_shared(step):
        share_copy(step).wait_recv()
        take_points(2 * chip_giver(step) + 1 - core)

    def take_sent(step):
        pts_copy(step).wait_recv()
        share_copy(step).start()
        take_points(2 * chip_giver(step) + core)

    take_shared(0)
    repeat(1, chips, take_sent)
    repeat(1, chips, take_shared)

    counts = sums[DEPTH * part : DEPTH * part + DEPTH, :]
    floor = jnp.maximum(counts, 1.0)
    occupied = (counts > 0).astype(jnp.float32)
    held = grid.shape[2]

    def grid_copy(chunk, step):
        planes = pl.ds(chunk * PER_CHUNK, PER_CHUNK)
        return pltpu.make_async_remote_copy(
            src_ref=grid.at[planes, mine],
            dst_ref=grid.at[planes, mine],
            send_sem=grid_send.at[chunk, step],
            recv_sem=grid_recv.at[chunk, step],
            device_id={"chan": chan_peer(step)},
        )

    chain = chans == 4
    inner = (mine == 1) | (mine == 2)

    def direct(step, act):
        if chain and step == 1:
            pl.when(mine != 3)(act)
        elif chain and step == 3:
            pl.when(mine != 0)(act)
        else:
            act()

    def relay_copy(chunk):
        planes = pl.ds(chunk * PER_CHUNK, PER_CHUNK)
        origin = lax.rem(mine + 2, chans)
        return pltpu.make_async_remote_copy(
            src_ref=grid.at[planes, origin],
            dst_ref=grid.at[planes, origin],
            send_sem=relay_send.at[chunk],
            recv_sem=grid_recv.at[chunk, jnp.where(mine == 1, 1, 3)],
            device_id={"chan": jnp.where(mine == 1, 0, 3)},
        )

    def pass_on(chunk):
        @pl.when(inner)
        def _():
            grid_copy(chunk, 2).wait_recv()
            relay_copy(chunk).start()

    for chunk in range(CHUNKS):
        for plane in range(chunk * PER_CHUNK, (chunk + 1) * PER_CHUNK):
            mean = sums[plane * part : (plane + 1) * part, :] / floor[plane : plane + 1, :]
            if held > part:
                mean = jnp.concatenate([mean, jnp.zeros((held - part, PLANE), jnp.float32)], axis=0)
            grid[plane, mine] = mean.astype(jnp.bfloat16)
        for step in (2, 1, 3) if chain else range(1, chans):
            direct(step, grid_copy(chunk, step).start)

    fetched[3].wait()
    for a in range(3):
        for tap in range(9):
            stacked[a * outs : (a + 1) * outs, tap * channels : (tap + 1) * channels] = weight_here[
                9 * a + tap
            ].astype(jnp.float32)
    for tap in range(9):
        place = slice(tap * channels, (tap + 1) * channels)
        taps[place, :] = stacked[:, place].T.astype(jnp.bfloat16)
    fetched[4].wait()
    for plane in range(DEPTH):
        kept = grad_here[:, plane * PLANE : (plane + 1) * PLANE].astype(jnp.float32)
        masked[plane + 1] = (kept * occupied[plane : plane + 1, :]).astype(jnp.bfloat16)

    def columns_of(plane):
        return jnp.concatenate(
            [moved[plane, b * EDGE : b * EDGE + PLANE, :] for b in range(3)], axis=1
        )

    def forward(plane, columns):
        partial[plane] = jnp.dot(columns, taps[...], preferred_element_type=jnp.float32).T

    if chain:
        pass_on(0)
    for chunk in range(CHUNKS):
        if chain and chunk + 1 < CHUNKS:
            pass_on(chunk + 1)
        for step in (1, 3) if chain else range(1, chans):
            grid_copy(chunk, step).wait_recv()
        if chain:
            pl.when(jnp.logical_not(inner))(grid_copy(chunk, 2).wait_recv)
        for plane in range(chunk * PER_CHUNK, (chunk + 1) * PER_CHUNK):
            if held > part:
                lanes = [grid[plane, c].astype(jnp.float32)[:part] for c in range(chans)]
                voxels = jnp.concatenate(lanes, axis=0).astype(jnp.bfloat16)
            else:
                voxels = grid[plane].reshape(channels, PLANE)
            lines = lax.dot_general(
                shifts[...], voxels, ROWS_MAJOR, preferred_element_type=jnp.float32
            ).astype(jnp.bfloat16)
            for e in range(3):
                moved[plane, EDGE : EDGE + PLANE, e * channels : (e + 1) * channels] = lines[
                    e * PLANE : (e + 1) * PLANE, :
                ]
            columns = columns_of(plane)
            if plane < DEPTH - LATE:
                forward(plane, columns)
            cotangents = jnp.concatenate([masked[plane + 2], masked[plane + 1], masked[plane]], axis=0)
            grads = jnp.dot(cotangents, columns, preferred_element_type=jnp.float32)
            for a in range(3):
                place = slice(a * 9 * channels, (a + 1) * 9 * channels)
                piece = grads[a * outs : (a + 1) * outs, :]
                if plane == 0:
                    total[:, place] = piece
                else:
                    total[:, place] += piece
    total[:, 27 * channels :] = jnp.zeros((outs, total.shape[1] - 27 * channels), jnp.float32)

    for owner in range(tiles):
        base, skip = owner * width // 128 * 128, owner * width % 128
        window = total[:, base : base + span + 128]
        if skip:
            window = pltpu.roll(window, span + 128 - skip, 1)
        blocks[owner] = window[:, :span]
        handing[owner] = window[:, :span].astype(jnp.bfloat16)

    def hand_copy(step):
        return pltpu.make_async_remote_copy(
            src_ref=handing.at[2 * chip_peer(step) + 1 - core],
            dst_ref=handed.at[step],
            send_sem=hand_send.at[step],
            recv_sem=hand_recv.at[step],
            device_id={"tile": sibling},
        )

    def grad_copy(step):
        return pltpu.make_async_remote_copy(
            src_ref=sending.at[step],
            dst_ref=received.at[step],
            send_sem=grad_send.at[step],
            recv_sem=grad_recv.at[step],
            device_id={"tile": 2 * chip_peer(step) + core},
        )

    repeat(1, chips, lambda step: hand_copy(step).start())
    hand_copy(0).start()

    def send_grads(step):
        hand_copy(step).wait_recv()
        both = blocks[2 * chip_peer(step) + core] + handed[step].astype(jnp.float32)
        sending[step] = both.astype(jnp.bfloat16)
        grad_copy(step).start()

    repeat(1, chips, send_grads)
    for plane in range(DEPTH - LATE, DEPTH):
        forward(plane, columns_of(plane))

    for plane in range(DEPTH):
        output = partial[plane, outs : 2 * outs, :]
        if plane > 0:
            output = output + partial[plane - 1, :outs, :]
        if plane < DEPTH - 1:
            output = output + partial[plane + 1, 2 * outs :, :]
        out_ref[:, plane * PLANE : (plane + 1) * PLANE] = (
            output * occupied[plane : plane + 1, :]
        ).astype(jnp.bfloat16)

    hand_copy(0).wait_recv()
    total[:, :span] = blocks[me] + handed[0].astype(jnp.float32)

    def take_grads(step):
        grad_copy(step).wait_recv()
        total[:, :span] += received[step].astype(jnp.float32)

    repeat(1, chips, take_grads)
    wgrad_ref[...] = total[:, :width]

    def sent(step):
        pts_copy(step).wait_send()
        grad_copy(step).wait_send()

    def handed_over(step):
        share_copy(step).wait_send()
        hand_copy(step).wait_send()

    repeat(1, tiles, lambda step: code_copy(step).wait_send())
    repeat(1, chips, sent)
    repeat(0, chips, handed_over)
    for chunk in range(CHUNKS):
        for step in range(1, chans):
            direct(step, grid_copy(chunk, step).wait_send)
        if chain:
            pl.when(inner)(relay_copy(chunk).wait_send)


def on_device(points, dest, voxel, weight, grad_out):
    tiles, chans = lax.axis_size("tile"), lax.axis_size("chan")
    part, count = points.shape
    outs = grad_out.shape[0]
    channels = part * chans
    width = 27 * channels // tiles
    span = -(-width // 128) * 128
    total_width = max(((tiles - 1) * width // 128) * 128 + span + 128, 27 * channels + 128)
    chips = tiles // 2
    hbm = pl.BlockSpec(memory_space=pltpu.HBM)
    vmem = pl.BlockSpec(memory_space=pltpu.VMEM)
    dma = pltpu.SemaphoreType.DMA
    return pl.pallas_call(
        functools.partial(kernel, tiles, chans, width),
        out_shape=(
            jax.ShapeDtypeStruct((outs, VOX), jnp.bfloat16),
            jax.ShapeDtypeStruct((outs, width), jnp.float32),
        ),
        in_specs=[hbm] * 5,
        out_specs=(vmem, vmem),
        scratch_shapes=[
            pltpu.VMEM((1, count), jnp.int32),
            pltpu.VMEM((1, count), jnp.int32),
            pltpu.VMEM((27, outs, channels), jnp.bfloat16),
            pltpu.VMEM((outs, VOX), jnp.bfloat16),
            pltpu.VMEM((tiles, 1, count), jnp.int32),
            pltpu.VMEM((tiles, part, count), jnp.bfloat16),
            pltpu.VMEM((DEPTH * part + 2 * DEPTH, PLANE), jnp.float32),
            pltpu.VMEM((DEPTH, chans, max(part, 16), PLANE), jnp.bfloat16),
            pltpu.VMEM((3 * PLANE, PLANE), jnp.bfloat16),
            pltpu.VMEM((DEPTH, PADDED, 3 * channels), jnp.bfloat16),
            pltpu.VMEM((3 * outs, 9 * channels), jnp.float32),
            pltpu.VMEM((9 * channels, 3 * outs), jnp.bfloat16),
            pltpu.VMEM((DEPTH + 2, outs, PLANE), jnp.bfloat16),
            pltpu.VMEM((DEPTH, 3 * outs, PLANE), jnp.float32),
            pltpu.VMEM((outs, total_width), jnp.float32),
            pltpu.VMEM((tiles, outs, span), jnp.float32),
            pltpu.VMEM((tiles, outs, span), jnp.bfloat16),
            pltpu.VMEM((chips, outs, span), jnp.bfloat16),
            pltpu.VMEM((chips, outs, span), jnp.bfloat16),
            pltpu.VMEM((chips, outs, span), jnp.bfloat16),
            dma((5,)),
            dma((chips,)),
            dma((chips,)),
            dma((chips,)),
            dma((chips,)),
            dma((tiles,)),
            dma((tiles,)),
            dma((CHUNKS, chans)),
            dma((CHUNKS, chans)),
            dma((CHUNKS,)),
            dma((chips,)),
            dma((chips,)),
            dma((chips,)),
            dma((chips,)),
        ],
        compiler_params=pltpu.CompilerParams(
            collective_id=0, has_side_effects=True, vmem_limit_bytes=48 * 1024 * 1024
        ),
    )(
        *(
            pltpu.with_memory_space_constraint(operand, pltpu.HBM)
            for operand in (
                points,
                dest.reshape(1, count),
                voxel.reshape(1, count),
                jnp.transpose(weight, (1, 0, 2)),
                grad_out,
            )
        )
    )


def solution(mesh):
    placed = (
        P("chan", "tile"),
        P("tile", None),
        P("tile", None),
        P("chan", None, None),
        P("chan", "tile"),
    )
    return jax.shard_map(
        on_device,
        mesh=mesh,
        in_specs=placed,
        out_specs=(P("chan", "tile"), P("chan", "tile")),
        check_vma=False,
    )
```

```python
import functools

import jax
import jax.numpy as jnp
from jax import lax
from jax.experimental import pallas as pl
from jax.experimental.pallas import tpu as pltpu
from jax.sharding import PartitionSpec as P

EDGE = 16
DEPTH = 8
PLANE = EDGE * EDGE
VOX = DEPTH * PLANE
PADDED = PLANE + 2 * EDGE
CHUNKS = 8
LATE = 6
PER_CHUNK = DEPTH // CHUNKS
ROWS_MAJOR = (((1,), (1,)), ((), ()))


def repeat(start, stop, body):
    if stop - start <= 8:
        for step in range(start, stop):
            body(step)
    else:
        lax.fori_loop(start, stop, lambda step, carry: (body(step), carry)[1], 0)


def kernel(
    tiles,
    chans,
    width,
    pts_ref,
    dest_ref,
    voxel_ref,
    weight_ref,
    grad_ref,
    out_ref,
    wgrad_ref,
    dest_here,
    voxel_here,
    weight_here,
    grad_here,
    codes,
    pts_all,
    sums,
    grid,
    shifts,
    moved,
    stacked,
    taps,
    masked,
    partial,
    total,
    blocks,
    handing,
    handed,
    sending,
    received,
    local_sem,
    pts_send,
    pts_recv,
    share_send,
    share_recv,
    code_send,
    code_recv,
    grid_send,
    grid_recv,
    relay_send,
    hand_send,
    hand_recv,
    grad_send,
    grad_recv,
):
    me = lax.axis_index("tile")
    mine = lax.axis_index("chan")
    part = pts_ref.shape[0]
    outs = grad_ref.shape[0]
    channels = part * chans
    span = sending.shape[2]
    chips = tiles // 2
    chip, core = me // 2, lax.rem(me, 2)
    sibling = 2 * chip + 1 - core

    def peer(step):
        return lax.rem(me + step, tiles)

    def giver(step):
        return lax.rem(me + tiles - step, tiles)

    def chip_peer(step):
        return lax.rem(chip + step, chips)

    def chip_giver(step):
        return lax.rem(chip + chips - step, chips)

    def chan_peer(step):
        return lax.rem(mine + step, chans)

    barrier = pltpu.get_barrier_semaphore()

    def greet(step):
        pl.semaphore_signal(barrier, inc=1, device_id={"tile": peer(step)})

    def greet_chan(step):
        pl.semaphore_signal(barrier, inc=1, device_id={"chan": chan_peer(step)})

    def local(place, source, target):
        return pltpu.make_async_copy(source, target, local_sem.at[place])

    fetched = [
        local(0, dest_ref, dest_here),
        local(1, voxel_ref, voxel_here),
        local(2, pts_ref, pts_all.at[me]),
        local(3, weight_ref, weight_here),
        local(4, grad_ref, grad_here),
    ]
    for copy in fetched:
        copy.start()
    repeat(1, tiles, greet)
    repeat(1, chans, greet_chan)
    fetched[0].wait()
    fetched[1].wait()
    codes[me] = dest_here[...] * VOX + voxel_here[...]
    pl.semaphore_wait(barrier, tiles + chans - 2)

    def code_copy(step):
        return pltpu.make_async_remote_copy(
            src_ref=codes.at[me],
            dst_ref=codes.at[me],
            send_sem=code_send.at[step],
            recv_sem=code_recv.at[step],
            device_id={"tile": peer(step)},
        )

    def pts_copy(step):
        return pltpu.make_async_remote_copy(
            src_ref=pts_ref,
            dst_ref=pts_all.at[me],
            send_sem=pts_send.at[step],
            recv_sem=pts_recv.at[step],
            device_id={"tile": 2 * chip_peer(step) + core},
        )

    def share_copy(step):
        origin = 2 * chip_giver(step) + core
        return pltpu.make_async_remote_copy(
            src_ref=pts_all.at[origin],
            dst_ref=pts_all.at[origin],
            send_sem=share_send.at[step],
            recv_sem=share_recv.at[step],
            device_id={"tile": sibling},
        )

    repeat(1, tiles, lambda step: code_copy(step).start())
    repeat(1, chips, lambda step: pts_copy(step).start())
    fetched[2].wait()
    share_copy(0).start()

    to = lax.broadcasted_iota(jnp.int32, (PLANE, PLANE), 0)
    source = lax.broadcasted_iota(jnp.int32, (PLANE, PLANE), 1)
    for e in (-1, 0, 1):
        line = (to & (EDGE - 1)) + e
        here = (source == to + e) & (line >= 0) & (line < EDGE)
        shifts[(e + 1) * PLANE : (e + 2) * PLANE, :] = here.astype(jnp.float32).astype(jnp.bfloat16)
    edge = jnp.zeros((EDGE, moved.shape[2]), jnp.bfloat16)
    for plane in range(DEPTH):
        moved[plane, :EDGE, :] = edge
        moved[plane, PADDED - EDGE :, :] = edge
    masked[0] = jnp.zeros((outs, PLANE), jnp.bfloat16)
    masked[DEPTH + 1] = jnp.zeros((outs, PLANE), jnp.bfloat16)

    def add_points(features, code):
        rel = code - me * VOX
        high = rel >> 8
        low = rel & (PLANE - 1)
        count = features.shape[1]
        wide = features.astype(jnp.float32)
        rows = [jnp.where(high == h, wide, 0.0).astype(jnp.bfloat16) for h in range(DEPTH)]
        rank = lax.broadcasted_iota(jnp.int32, (2 * DEPTH, count), 0)
        rows.append((rank == high).astype(jnp.float32).astype(jnp.bfloat16))
        cell = lax.broadcasted_iota(jnp.int32, (PLANE, count), 0)
        onehot = (cell == low).astype(jnp.float32).astype(jnp.bfloat16)
        return lax.dot_general(
            jnp.concatenate(rows, axis=0), onehot, ROWS_MAJOR, preferred_element_type=jnp.float32
        )

    sums[...] = add_points(pts_all[me], codes[me])
    repeat(1, tiles, lambda step: code_copy(step).wait_recv())

    def take_points(origin):
        sums[...] += add_points(pts_all[origin], codes[origin])

    def take_shared(step):
        share_copy(step).wait_recv()
        take_points(2 * chip_giver(step) + 1 - core)

    def pass_points(step):
        pts_copy(step).wait_recv()
        share_copy(step).start()

    def take_sent(step):
        take_points(2 * chip_giver(step) + core)

    take_shared(0)
    repeat(1, chips, pass_points)
    repeat(1, chips, take_sent)
    repeat(1, chips, take_shared)

    counts = sums[DEPTH * part : DEPTH * part + DEPTH, :]
    floor = jnp.maximum(counts, 1.0)
    occupied = (counts > 0).astype(jnp.float32)
    held = grid.shape[2]

    def grid_copy(chunk, step):
        planes = pl.ds(chunk * PER_CHUNK, PER_CHUNK)
        return pltpu.make_async_remote_copy(
            src_ref=grid.at[planes, mine],
            dst_ref=grid.at[planes, mine],
            send_sem=grid_send.at[chunk, step],
            recv_sem=grid_recv.at[chunk, step],
            device_id={"chan": chan_peer(step)},
        )

    chain = chans == 4
    inner = (mine == 1) | (mine == 2)

    def direct(step, act):
        if chain and step == 1:
            pl.when(mine != 3)(act)
        elif chain and step == 3:
            pl.when(mine != 0)(act)
        else:
            act()

    def relay_copy(chunk):
        planes = pl.ds(chunk * PER_CHUNK, PER_CHUNK)
        origin = lax.rem(mine + 2, chans)
        return pltpu.make_async_remote_copy(
            src_ref=grid.at[planes, origin],
            dst_ref=grid.at[planes, origin],
            send_sem=relay_send.at[chunk],
            recv_sem=grid_recv.at[chunk, jnp.where(mine == 1, 1, 3)],
            device_id={"chan": jnp.where(mine == 1, 0, 3)},
        )

    def pass_on(chunk):
        @pl.when(inner)
        def _():
            grid_copy(chunk, 2).wait_recv()
            relay_copy(chunk).start()

    for chunk in range(CHUNKS):
        for plane in range(chunk * PER_CHUNK, (chunk + 1) * PER_CHUNK):
            mean = sums[plane * part : (plane + 1) * part, :] / floor[plane : plane + 1, :]
            if held > part:
                mean = jnp.concatenate([mean, jnp.zeros((held - part, PLANE), jnp.float32)], axis=0)
            grid[plane, mine] = mean.astype(jnp.bfloat16)
        for step in (2, 1, 3) if chain else range(1, chans):
            direct(step, grid_copy(chunk, step).start)

    fetched[3].wait()
    for a in range(3):
        for tap in range(9):
            stacked[a * outs : (a + 1) * outs, tap * channels : (tap + 1) * channels] = weight_here[
                9 * a + tap
            ].astype(jnp.float32)
    for tap in range(9):
        place = slice(tap * channels, (tap + 1) * channels)
        taps[place, :] = stacked[:, place].T.astype(jnp.bfloat16)
    fetched[4].wait()
    for plane in range(DEPTH):
        kept = grad_here[:, plane * PLANE : (plane + 1) * PLANE].astype(jnp.float32)
        masked[plane + 1] = (kept * occupied[plane : plane + 1, :]).astype(jnp.bfloat16)

    def columns_of(plane):
        return jnp.concatenate(
            [moved[plane, b * EDGE : b * EDGE + PLANE, :] for b in range(3)], axis=1
        )

    def forward(plane, columns):
        partial[plane] = jnp.dot(columns, taps[...], preferred_element_type=jnp.float32).T

    if chain:
        pass_on(0)
    for chunk in range(CHUNKS):
        if chain and chunk + 1 < CHUNKS:
            pass_on(chunk + 1)
        for step in (1, 3) if chain else range(1, chans):
            grid_copy(chunk, step).wait_recv()
        if chain:
            pl.when(jnp.logical_not(inner))(grid_copy(chunk, 2).wait_recv)
        for plane in range(chunk * PER_CHUNK, (chunk + 1) * PER_CHUNK):
            if held > part:
                lanes = [grid[plane, c].astype(jnp.float32)[:part] for c in range(chans)]
                voxels = jnp.concatenate(lanes, axis=0).astype(jnp.bfloat16)
            else:
                voxels = grid[plane].reshape(channels, PLANE)
            lines = lax.dot_general(
                shifts[...], voxels, ROWS_MAJOR, preferred_element_type=jnp.float32
            ).astype(jnp.bfloat16)
            for e in range(3):
                moved[plane, EDGE : EDGE + PLANE, e * channels : (e + 1) * channels] = lines[
                    e * PLANE : (e + 1) * PLANE, :
                ]
            columns = columns_of(plane)
            if plane < DEPTH - LATE:
                forward(plane, columns)
            cotangents = jnp.concatenate([masked[plane + 2], masked[plane + 1], masked[plane]], axis=0)
            grads = jnp.dot(cotangents, columns, preferred_element_type=jnp.float32)
            for a in range(3):
                place = slice(a * 9 * channels, (a + 1) * 9 * channels)
                piece = grads[a * outs : (a + 1) * outs, :]
                if plane == 0:
                    total[:, place] = piece
                else:
                    total[:, place] += piece
    total[:, 27 * channels :] = jnp.zeros((outs, total.shape[1] - 27 * channels), jnp.float32)

    for owner in range(tiles):
        base, skip = owner * width // 128 * 128, owner * width % 128
        window = total[:, base : base + span + 128]
        if skip:
            window = pltpu.roll(window, span + 128 - skip, 1)
        blocks[owner] = window[:, :span]
        handing[owner] = window[:, :span].astype(jnp.bfloat16)

    def hand_copy(step):
        return pltpu.make_async_remote_copy(
            src_ref=handing.at[2 * chip_peer(step) + 1 - core],
            dst_ref=handed.at[step],
            send_sem=hand_send.at[step],
            recv_sem=hand_recv.at[step],
            device_id={"tile": sibling},
        )

    def grad_copy(step):
        return pltpu.make_async_remote_copy(
            src_ref=sending.at[step],
            dst_ref=received.at[step],
            send_sem=grad_send.at[step],
            recv_sem=grad_recv.at[step],
            device_id={"tile": 2 * chip_peer(step) + core},
        )

    repeat(1, chips, lambda step: hand_copy(step).start())
    hand_copy(0).start()

    def send_grads(step):
        hand_copy(step).wait_recv()
        both = blocks[2 * chip_peer(step) + core] + handed[step].astype(jnp.float32)
        sending[step] = both.astype(jnp.bfloat16)
        grad_copy(step).start()

    repeat(1, chips, send_grads)
    for plane in range(DEPTH - LATE, DEPTH):
        forward(plane, columns_of(plane))

    for plane in range(DEPTH):
        output = partial[plane, outs : 2 * outs, :]
        if plane > 0:
            output = output + partial[plane - 1, :outs, :]
        if plane < DEPTH - 1:
            output = output + partial[plane + 1, 2 * outs :, :]
        out_ref[:, plane * PLANE : (plane + 1) * PLANE] = (
            output * occupied[plane : plane + 1, :]
        ).astype(jnp.bfloat16)

    hand_copy(0).wait_recv()
    total[:, :span] = blocks[me] + handed[0].astype(jnp.float32)

    def take_grads(step):
        grad_copy(step).wait_recv()
        total[:, :span] += received[step].astype(jnp.float32)

    repeat(1, chips, take_grads)
    wgrad_ref[...] = total[:, :width]

    def sent(step):
        pts_copy(step).wait_send()
        grad_copy(step).wait_send()

    def handed_over(step):
        share_copy(step).wait_send()
        hand_copy(step).wait_send()

    repeat(1, tiles, lambda step: code_copy(step).wait_send())
    repeat(1, chips, sent)
    repeat(0, chips, handed_over)
    for chunk in range(CHUNKS):
        for step in range(1, chans):
            direct(step, grid_copy(chunk, step).wait_send)
        if chain:
            pl.when(inner)(relay_copy(chunk).wait_send)


def on_device(points, dest, voxel, weight, grad_out):
    tiles, chans = lax.axis_size("tile"), lax.axis_size("chan")
    part, count = points.shape
    outs = grad_out.shape[0]
    channels = part * chans
    width = 27 * channels // tiles
    span = -(-width // 128) * 128
    total_width = max(((tiles - 1) * width // 128) * 128 + span + 128, 27 * channels + 128)
    chips = tiles // 2
    hbm = pl.BlockSpec(memory_space=pltpu.HBM)
    vmem = pl.BlockSpec(memory_space=pltpu.VMEM)
    dma = pltpu.SemaphoreType.DMA
    return pl.pallas_call(
        functools.partial(kernel, tiles, chans, width),
        out_shape=(
            jax.ShapeDtypeStruct((outs, VOX), jnp.bfloat16),
            jax.ShapeDtypeStruct((outs, width), jnp.float32),
        ),
        in_specs=[hbm] * 5,
        out_specs=(vmem, vmem),
        scratch_shapes=[
            pltpu.VMEM((1, count), jnp.int32),
            pltpu.VMEM((1, count), jnp.int32),
            pltpu.VMEM((27, outs, channels), jnp.bfloat16),
            pltpu.VMEM((outs, VOX), jnp.bfloat16),
            pltpu.VMEM((tiles, 1, count), jnp.int32),
            pltpu.VMEM((tiles, part, count), jnp.bfloat16),
            pltpu.VMEM((DEPTH * part + 2 * DEPTH, PLANE), jnp.float32),
            pltpu.VMEM((DEPTH, chans, max(part, 16), PLANE), jnp.bfloat16),
            pltpu.VMEM((3 * PLANE, PLANE), jnp.bfloat16),
            pltpu.VMEM((DEPTH, PADDED, 3 * channels), jnp.bfloat16),
            pltpu.VMEM((3 * outs, 9 * channels), jnp.float32),
            pltpu.VMEM((9 * channels, 3 * outs), jnp.bfloat16),
            pltpu.VMEM((DEPTH + 2, outs, PLANE), jnp.bfloat16),
            pltpu.VMEM((DEPTH, 3 * outs, PLANE), jnp.float32),
            pltpu.VMEM((outs, total_width), jnp.float32),
            pltpu.VMEM((tiles, outs, span), jnp.float32),
            pltpu.VMEM((tiles, outs, span), jnp.bfloat16),
            pltpu.VMEM((chips, outs, span), jnp.bfloat16),
            pltpu.VMEM((chips, outs, span), jnp.bfloat16),
            pltpu.VMEM((chips, outs, span), jnp.bfloat16),
            dma((5,)),
            dma((chips,)),
            dma((chips,)),
            dma((chips,)),
            dma((chips,)),
            dma((tiles,)),
            dma((tiles,)),
            dma((CHUNKS, chans)),
            dma((CHUNKS, chans)),
            dma((CHUNKS,)),
            dma((chips,)),
            dma((chips,)),
            dma((chips,)),
            dma((chips,)),
        ],
        compiler_params=pltpu.CompilerParams(
            collective_id=0, has_side_effects=True, vmem_limit_bytes=48 * 1024 * 1024
        ),
    )(
        *(
            pltpu.with_memory_space_constraint(operand, pltpu.HBM)
            for operand in (
                points,
                dest.reshape(1, count),
                voxel.reshape(1, count),
                jnp.transpose(weight, (1, 0, 2)),
                grad_out,
            )
        )
    )


def solution(mesh):
    placed = (
        P("chan", "tile"),
        P("tile", None),
        P("tile", None),
        P("chan", None, None),
        P("chan", "tile"),
    )
    return jax.shard_map(
        on_device,
        mesh=mesh,
        in_specs=placed,
        out_specs=(P("chan", "tile"), P("chan", "tile")),
        check_vma=False,
    )
```

```python
import functools

import jax
import jax.numpy as jnp
from jax import lax
from jax.experimental import pallas as pl
from jax.experimental.pallas import tpu as pltpu
from jax.sharding import PartitionSpec as P

EDGE = 16
DEPTH = 8
PLANE = EDGE * EDGE
VOX = DEPTH * PLANE
PADDED = PLANE + 2 * EDGE
CHUNKS = 8
LATE = 8
PER_CHUNK = DEPTH // CHUNKS
ROWS_MAJOR = (((1,), (1,)), ((), ()))


def repeat(start, stop, body):
    if stop - start <= 8:
        for step in range(start, stop):
            body(step)
    else:
        lax.fori_loop(start, stop, lambda step, carry: (body(step), carry)[1], 0)


def kernel(
    tiles,
    chans,
    width,
    pts_ref,
    dest_ref,
    voxel_ref,
    weight_ref,
    grad_ref,
    out_ref,
    wgrad_ref,
    dest_here,
    voxel_here,
    weight_here,
    grad_here,
    codes,
    pts_all,
    sums,
    grid,
    shifts,
    moved,
    stacked,
    taps,
    masked,
    partial,
    total,
    blocks,
    handing,
    handed,
    sending,
    received,
    local_sem,
    pts_send,
    pts_recv,
    share_send,
    share_recv,
    code_send,
    code_recv,
    grid_send,
    grid_recv,
    relay_send,
    hand_send,
    hand_recv,
    grad_send,
    grad_recv,
):
    me = lax.axis_index("tile")
    mine = lax.axis_index("chan")
    part = pts_ref.shape[0]
    outs = grad_ref.shape[0]
    channels = part * chans
    span = sending.shape[2]
    chips = tiles // 2
    chip, core = me // 2, lax.rem(me, 2)
    sibling = 2 * chip + 1 - core

    def peer(step):
        return lax.rem(me + step, tiles)

    def giver(step):
        return lax.rem(me + tiles - step, tiles)

    def chip_peer(step):
        return lax.rem(chip + step, chips)

    def chip_giver(step):
        return lax.rem(chip + chips - step, chips)

    def chan_peer(step):
        return lax.rem(mine + step, chans)

    barrier = pltpu.get_barrier_semaphore()

    def greet(step):
        pl.semaphore_signal(barrier, inc=1, device_id={"tile": peer(step)})

    def greet_chan(step):
        pl.semaphore_signal(barrier, inc=1, device_id={"chan": chan_peer(step)})

    def local(place, source, target):
        return pltpu.make_async_copy(source, target, local_sem.at[place])

    fetched = [
        local(0, dest_ref, dest_here),
        local(1, voxel_ref, voxel_here),
        local(2, pts_ref, pts_all.at[me]),
        local(3, weight_ref, weight_here),
        local(4, grad_ref, grad_here),
    ]
    for copy in fetched:
        copy.start()
    repeat(1, tiles, greet)
    repeat(1, chans, greet_chan)
    fetched[0].wait()
    fetched[1].wait()
    codes[me] = dest_here[...] * VOX + voxel_here[...]
    pl.semaphore_wait(barrier, tiles + chans - 2)

    def code_copy(step):
        return pltpu.make_async_remote_copy(
            src_ref=codes.at[me],
            dst_ref=codes.at[me],
            send_sem=code_send.at[step],
            recv_sem=code_recv.at[step],
            device_id={"tile": peer(step)},
        )

    def pts_copy(step):
        return pltpu.make_async_remote_copy(
            src_ref=pts_ref,
            dst_ref=pts_all.at[me],
            send_sem=pts_send.at[step],
            recv_sem=pts_recv.at[step],
            device_id={"tile": 2 * chip_peer(step) + core},
        )

    def share_copy(step):
        origin = 2 * chip_giver(step) + core
        return pltpu.make_async_remote_copy(
            src_ref=pts_all.at[origin],
            dst_ref=pts_all.at[origin],
            send_sem=share_send.at[step],
            recv_sem=share_recv.at[step],
            device_id={"tile": sibling},
        )

    repeat(1, tiles, lambda step: code_copy(step).start())
    repeat(1, chips, lambda step: pts_copy(step).start())
    fetched[2].wait()
    share_copy(0).start()

    to = lax.broadcasted_iota(jnp.int32, (PLANE, PLANE), 0)
    source = lax.broadcasted_iota(jnp.int32, (PLANE, PLANE), 1)
    for e in (-1, 0, 1):
        line = (to & (EDGE - 1)) + e
        here = (source == to + e) & (line >= 0) & (line < EDGE)
        shifts[(e + 1) * PLANE : (e + 2) * PLANE, :] = here.astype(jnp.float32).astype(jnp.bfloat16)
    edge = jnp.zeros((EDGE, moved.shape[2]), jnp.bfloat16)
    for plane in range(DEPTH):
        moved[plane, :EDGE, :] = edge
        moved[plane, PADDED - EDGE :, :] = edge
    masked[0] = jnp.zeros((outs, PLANE), jnp.bfloat16)
    masked[DEPTH + 1] = jnp.zeros((outs, PLANE), jnp.bfloat16)

    def add_points(features, code):
        rel = code - me * VOX
        high = rel >> 8
        low = rel & (PLANE - 1)
        count = features.shape[1]
        wide = features.astype(jnp.float32)
        rows = [jnp.where(high == h, wide, 0.0).astype(jnp.bfloat16) for h in range(DEPTH)]
        rank = lax.broadcasted_iota(jnp.int32, (2 * DEPTH, count), 0)
        rows.append((rank == high).astype(jnp.float32).astype(jnp.bfloat16))
        cell = lax.broadcasted_iota(jnp.int32, (PLANE, count), 0)
        onehot = (cell == low).astype(jnp.float32).astype(jnp.bfloat16)
        return lax.dot_general(
            jnp.concatenate(rows, axis=0), onehot, ROWS_MAJOR, preferred_element_type=jnp.float32
        )

    sums[...] = add_points(pts_all[me], codes[me])
    repeat(1, tiles, lambda step: code_copy(step).wait_recv())

    def take_points(origin):
        sums[...] += add_points(pts_all[origin], codes[origin])

    def take_shared(step):
        share_copy(step).wait_recv()
        take_points(2 * chip_giver(step) + 1 - core)

    def pass_points(step):
        pts_copy(step).wait_recv()
        share_copy(step).start()

    def take_sent(step):
        take_points(2 * chip_giver(step) + core)

    take_shared(0)
    repeat(1, chips, pass_points)
    repeat(1, chips, take_sent)
    repeat(1, chips, take_shared)

    counts = sums[DEPTH * part : DEPTH * part + DEPTH, :]
    floor = jnp.maximum(counts, 1.0)
    occupied = (counts > 0).astype(jnp.float32)
    held = grid.shape[2]

    def grid_copy(chunk, step):
        planes = pl.ds(chunk * PER_CHUNK, PER_CHUNK)
        return pltpu.make_async_remote_copy(
            src_ref=grid.at[planes, mine],
            dst_ref=grid.at[planes, mine],
            send_sem=grid_send.at[chunk, step],
            recv_sem=grid_recv.at[chunk, step],
            device_id={"chan": chan_peer(step)},
        )

    chain = chans == 4
    inner = (mine == 1) | (mine == 2)

    def direct(step, act):
        if chain and step == 1:
            pl.when(mine != 3)(act)
        elif chain and step == 3:
            pl.when(mine != 0)(act)
        else:
            act()

    def relay_copy(chunk):
        planes = pl.ds(chunk * PER_CHUNK, PER_CHUNK)
        origin = lax.rem(mine + 2, chans)
        return pltpu.make_async_remote_copy(
            src_ref=grid.at[planes, origin],
            dst_ref=grid.at[planes, origin],
            send_sem=relay_send.at[chunk],
            recv_sem=grid_recv.at[chunk, jnp.where(mine == 1, 1, 3)],
            device_id={"chan": jnp.where(mine == 1, 0, 3)},
        )

    def pass_on(chunk):
        @pl.when(inner)
        def _():
            grid_copy(chunk, 2).wait_recv()
            relay_copy(chunk).start()

    for chunk in range(CHUNKS):
        for plane in range(chunk * PER_CHUNK, (chunk + 1) * PER_CHUNK):
            mean = sums[plane * part : (plane + 1) * part, :] / floor[plane : plane + 1, :]
            if held > part:
                mean = jnp.concatenate([mean, jnp.zeros((held - part, PLANE), jnp.float32)], axis=0)
            grid[plane, mine] = mean.astype(jnp.bfloat16)
        for step in (2, 1, 3) if chain else range(1, chans):
            direct(step, grid_copy(chunk, step).start)

    fetched[3].wait()
    for a in range(3):
        for tap in range(9):
            stacked[a * outs : (a + 1) * outs, tap * channels : (tap + 1) * channels] = weight_here[
                9 * a + tap
            ].astype(jnp.float32)
    for tap in range(9):
        place = slice(tap * channels, (tap + 1) * channels)
        taps[place, :] = stacked[:, place].T.astype(jnp.bfloat16)
    fetched[4].wait()
    for plane in range(DEPTH):
        kept = grad_here[:, plane * PLANE : (plane + 1) * PLANE].astype(jnp.float32)
        masked[plane + 1] = (kept * occupied[plane : plane + 1, :]).astype(jnp.bfloat16)

    def columns_of(plane):
        return jnp.concatenate(
            [moved[plane, b * EDGE : b * EDGE + PLANE, :] for b in range(3)], axis=1
        )

    def forward(plane, columns):
        partial[plane] = jnp.dot(columns, taps[...], preferred_element_type=jnp.float32).T

    if chain:
        pass_on(0)
    for chunk in range(CHUNKS):
        if chain and chunk + 1 < CHUNKS:
            pass_on(chunk + 1)
        for step in (1, 3) if chain else range(1, chans):
            grid_copy(chunk, step).wait_recv()
        if chain:
            pl.when(jnp.logical_not(inner))(grid_copy(chunk, 2).wait_recv)
        for plane in range(chunk * PER_CHUNK, (chunk + 1) * PER_CHUNK):
            if held > part:
                lanes = [grid[plane, c].astype(jnp.float32)[:part] for c in range(chans)]
                voxels = jnp.concatenate(lanes, axis=0).astype(jnp.bfloat16)
            else:
                voxels = grid[plane].reshape(channels, PLANE)
            lines = lax.dot_general(
                shifts[...], voxels, ROWS_MAJOR, preferred_element_type=jnp.float32
            ).astype(jnp.bfloat16)
            for e in range(3):
                moved[plane, EDGE : EDGE + PLANE, e * channels : (e + 1) * channels] = lines[
                    e * PLANE : (e + 1) * PLANE, :
                ]
            columns = columns_of(plane)
            if plane < DEPTH - LATE:
                forward(plane, columns)
            cotangents = jnp.concatenate([masked[plane + 2], masked[plane + 1], masked[plane]], axis=0)
            grads = jnp.dot(cotangents, columns, preferred_element_type=jnp.float32)
            for a in range(3):
                place = slice(a * 9 * channels, (a + 1) * 9 * channels)
                piece = grads[a * outs : (a + 1) * outs, :]
                if plane == 0:
                    total[:, place] = piece
                else:
                    total[:, place] += piece
    total[:, 27 * channels :] = jnp.zeros((outs, total.shape[1] - 27 * channels), jnp.float32)

    for owner in range(tiles):
        base, skip = owner * width // 128 * 128, owner * width % 128
        window = total[:, base : base + span + 128]
        if skip:
            window = pltpu.roll(window, span + 128 - skip, 1)
        blocks[owner] = window[:, :span]
        handing[owner] = window[:, :span].astype(jnp.bfloat16)

    def hand_copy(step):
        return pltpu.make_async_remote_copy(
            src_ref=handing.at[2 * chip_peer(step) + 1 - core],
            dst_ref=handed.at[step],
            send_sem=hand_send.at[step],
            recv_sem=hand_recv.at[step],
            device_id={"tile": sibling},
        )

    def grad_copy(step):
        return pltpu.make_async_remote_copy(
            src_ref=sending.at[step],
            dst_ref=received.at[step],
            send_sem=grad_send.at[step],
            recv_sem=grad_recv.at[step],
            device_id={"tile": 2 * chip_peer(step) + core},
        )

    repeat(1, chips, lambda step: hand_copy(step).start())
    hand_copy(0).start()

    def send_grads(step):
        hand_copy(step).wait_recv()
        both = blocks[2 * chip_peer(step) + core] + handed[step].astype(jnp.float32)
        sending[step] = both.astype(jnp.bfloat16)
        grad_copy(step).start()

    repeat(1, chips, send_grads)
    for plane in range(DEPTH - LATE, DEPTH):
        forward(plane, columns_of(plane))

    for plane in range(DEPTH):
        output = partial[plane, outs : 2 * outs, :]
        if plane > 0:
            output = output + partial[plane - 1, :outs, :]
        if plane < DEPTH - 1:
            output = output + partial[plane + 1, 2 * outs :, :]
        out_ref[:, plane * PLANE : (plane + 1) * PLANE] = (
            output * occupied[plane : plane + 1, :]
        ).astype(jnp.bfloat16)

    hand_copy(0).wait_recv()
    total[:, :span] = blocks[me] + handed[0].astype(jnp.float32)

    def take_grads(step):
        grad_copy(step).wait_recv()
        total[:, :span] += received[step].astype(jnp.float32)

    repeat(1, chips, take_grads)
    wgrad_ref[...] = total[:, :width]

    def sent(step):
        pts_copy(step).wait_send()
        grad_copy(step).wait_send()

    def handed_over(step):
        share_copy(step).wait_send()
        hand_copy(step).wait_send()

    repeat(1, tiles, lambda step: code_copy(step).wait_send())
    repeat(1, chips, sent)
    repeat(0, chips, handed_over)
    for chunk in range(CHUNKS):
        for step in range(1, chans):
            direct(step, grid_copy(chunk, step).wait_send)
        if chain:
            pl.when(inner)(relay_copy(chunk).wait_send)


def on_device(points, dest, voxel, weight, grad_out):
    tiles, chans = lax.axis_size("tile"), lax.axis_size("chan")
    part, count = points.shape
    outs = grad_out.shape[0]
    channels = part * chans
    width = 27 * channels // tiles
    span = -(-width // 128) * 128
    total_width = max(((tiles - 1) * width // 128) * 128 + span + 128, 27 * channels + 128)
    chips = tiles // 2
    hbm = pl.BlockSpec(memory_space=pltpu.HBM)
    vmem = pl.BlockSpec(memory_space=pltpu.VMEM)
    dma = pltpu.SemaphoreType.DMA
    return pl.pallas_call(
        functools.partial(kernel, tiles, chans, width),
        out_shape=(
            jax.ShapeDtypeStruct((outs, VOX), jnp.bfloat16),
            jax.ShapeDtypeStruct((outs, width), jnp.float32),
        ),
        in_specs=[hbm] * 5,
        out_specs=(vmem, vmem),
        scratch_shapes=[
            pltpu.VMEM((1, count), jnp.int32),
            pltpu.VMEM((1, count), jnp.int32),
            pltpu.VMEM((27, outs, channels), jnp.bfloat16),
            pltpu.VMEM((outs, VOX), jnp.bfloat16),
            pltpu.VMEM((tiles, 1, count), jnp.int32),
            pltpu.VMEM((tiles, part, count), jnp.bfloat16),
            pltpu.VMEM((DEPTH * part + 2 * DEPTH, PLANE), jnp.float32),
            pltpu.VMEM((DEPTH, chans, max(part, 16), PLANE), jnp.bfloat16),
            pltpu.VMEM((3 * PLANE, PLANE), jnp.bfloat16),
            pltpu.VMEM((DEPTH, PADDED, 3 * channels), jnp.bfloat16),
            pltpu.VMEM((3 * outs, 9 * channels), jnp.float32),
            pltpu.VMEM((9 * channels, 3 * outs), jnp.bfloat16),
            pltpu.VMEM((DEPTH + 2, outs, PLANE), jnp.bfloat16),
            pltpu.VMEM((DEPTH, 3 * outs, PLANE), jnp.float32),
            pltpu.VMEM((outs, total_width), jnp.float32),
            pltpu.VMEM((tiles, outs, span), jnp.float32),
            pltpu.VMEM((tiles, outs, span), jnp.bfloat16),
            pltpu.VMEM((chips, outs, span), jnp.bfloat16),
            pltpu.VMEM((chips, outs, span), jnp.bfloat16),
            pltpu.VMEM((chips, outs, span), jnp.bfloat16),
            dma((5,)),
            dma((chips,)),
            dma((chips,)),
            dma((chips,)),
            dma((chips,)),
            dma((tiles,)),
            dma((tiles,)),
            dma((CHUNKS, chans)),
            dma((CHUNKS, chans)),
            dma((CHUNKS,)),
            dma((chips,)),
            dma((chips,)),
            dma((chips,)),
            dma((chips,)),
        ],
        compiler_params=pltpu.CompilerParams(
            collective_id=0, has_side_effects=True, vmem_limit_bytes=48 * 1024 * 1024
        ),
    )(
        *(
            pltpu.with_memory_space_constraint(operand, pltpu.HBM)
            for operand in (
                points,
                dest.reshape(1, count),
                voxel.reshape(1, count),
                jnp.transpose(weight, (1, 0, 2)),
                grad_out,
            )
        )
    )


def solution(mesh):
    placed = (
        P("chan", "tile"),
        P("tile", None),
        P("tile", None),
        P("chan", None, None),
        P("chan", "tile"),
    )
    return jax.shard_map(
        on_device,
        mesh=mesh,
        in_specs=placed,
        out_specs=(P("chan", "tile"), P("chan", "tile")),
        check_vma=False,
    )
```
